128 devices in a mesh: dp: 16 (over x, z), row: 4 (over y_hi, core), col: 2 (over y_lo).
Axes of the slice: x: 4, y: 4 (y_hi: 2, y_lo: 2; y = y_hi * 2 + y_lo), z: 4, core: 2. Of those that a mesh axis runs over, the one named last changes fastest.
Arguments:
- atom_feats: bfloat16 [2, 1024, 32, 1024], P(None, 'dp'), may hold values from -6 to 6
- atom_bead: int32 [2, 1024, 32], P(None, 'dp'), may hold values from 0 to 15, as said below
- bead_count: int32 [2, 1024], P(None, 'dp'), may hold values from 8 to 16
- bead_type: int32 [2, 1024, 16], P(None, 'dp'), may hold values from 0 to 3
- sparse_points: bfloat16 [8192, 1024], P(('row', 'col')), may hold values from -6 to 6
- sparse_type: int32 [8192], P(('row', 'col')), may hold values from 0 to 3
- targets: float32 [2, 3, 1024], P(None, None, 'dp'), may hold values from -6 to 6
Outputs:
- gram: float32 [8192, 4, 2048], P(('row', 'dp'), None, 'col')
- rhs: float32 [3, 8192], P(None, ('row', 'col'))
The draws below stay inside these ranges and needn't reach their ends.
Inputs may be any that keep to these rules, and one draw needn't show every extreme that they name: `atom_bead`: in every configuration the atoms map to beads below its bead count, and every bead below the count holds at least one atom.
All inputs are finite; a program needn't handle non-finite values.
Results may differ from the reference program's by a relative error of at most 0.012.
Values may be sent and summed in bfloat16 or wider, within the bound.
A program may use at most 128 MiB of HBM per device.

```python
import jax
import jax.numpy as jnp
from jax import lax

D = 1024
M = 8192
BEADS = 16
ATOMS = 32
TYPES = 4
SLABS = 2
CONF = 1024
TOTAL = 2048
N_ROW = 4


def shared_counts(key):
    drawn = jax.random.randint(key, (SLABS, CONF), BEADS // 2, BEADS + 1)
    position = jnp.arange(CONF, dtype=jnp.int32)[None, :]
    drawn = jnp.where(position % 8 == 0, BEADS, drawn)
    drawn = jnp.where(position % 8 == 1, BEADS // 2, drawn)
    return drawn.astype(jnp.int32)


def draw_bead_count(key, part):
    return shared_counts(key)


def draw_atom_bead(key, part):
    counts = shared_counts(key)
    key = jax.random.fold_in(key, 7)
    extra = jax.random.randint(key, (SLABS, CONF, ATOMS), 0, counts[:, :, None])
    order = jnp.arange(ATOMS, dtype=jnp.int32)[None, None, :]
    return jnp.where(order < counts[:, :, None], order, extra).astype(jnp.int32)


def place_ends(array, stream_key, least, largest):
    extent = array.shape
    place = [jax.random.randint(jax.random.fold_in(stream_key, axis), (), 0, extent[axis]) for axis in range(len(extent))]
    array = array.at[tuple(place)].set(least)
    longest = extent.index(max(extent))
    place[longest] = (place[longest] + 1) % extent[longest]
    return array.at[tuple(place)].set(largest)


def shard_levels(stream_key, extent, shards, least, largest):
    gain, own = 1.0, jax.random.fold_in(stream_key, 6)
    for dim, blocks in shards:
        steps = jnp.exp(jax.random.uniform(jax.random.fold_in(own, dim), (blocks,), jnp.float32, least / len(shards), largest / len(shards)))
        gain = gain * jnp.repeat(steps, extent[dim] // blocks).reshape([-1 if axis == dim else 1 for axis in range(len(extent))])
    return gain


def gaussian(rng, dims, spread, reach, shards=(), held_as=jnp.bfloat16):
    values = spread * jax.random.normal(rng, dims, jnp.float32)
    if shards:
        values = values * shard_levels(rng, dims, shards, -0.22, 0.18)
    return jnp.clip(values, -reach, reach).astype(held_as)


def setup_inputs(seed: int = 0) -> dict:
    streams_of = jax.random.split(jax.random.key(seed), 8)
    return {
        "atom_feats": gaussian(streams_of[0], (SLABS, CONF, ATOMS, D), 1.0, 6.0, ((1, 16),)),
        "atom_bead": draw_atom_bead(jax.random.fold_in(streams_of[7], 71), 0),
        "bead_count": draw_bead_count(jax.random.fold_in(streams_of[7], 71), 0),
        "bead_type": place_ends(jax.random.randint(streams_of[3], (SLABS, CONF, BEADS), 0, TYPES), jax.random.fold_in(streams_of[3], 1), 0, TYPES - 1).astype(jnp.int32),
        "sparse_points": gaussian(streams_of[4], (M, D), 1.0, 6.0, ((0, 8),)),
        "sparse_type": place_ends(jax.random.randint(streams_of[5], (M,), 0, TYPES), jax.random.fold_in(streams_of[5], 1), 0, TYPES - 1).astype(jnp.int32),
        "targets": gaussian(streams_of[6], (SLABS, 3, CONF), 1.0, 6.0, ((2, 16),), jnp.float32),
    }


EPSILON = 1e-06

def unit_rows(values):
    widened = values.astype(jnp.float32)
    scale = jnp.sqrt(lax.optimization_barrier(jnp.mean(widened * widened, axis=-1, keepdims=True)) + EPSILON)
    return (widened / scale).astype(jnp.bfloat16)

def bead_units(atom_feats, atom_bead):
    slots = jnp.arange(BEADS, dtype=jnp.int32)
    onehot = (atom_bead[:, None, :] == slots[None, :, None]).astype(jnp.float32)
    summed = jnp.einsum('gba,gad->gbd', onehot, atom_feats.astype(jnp.float32))
    bead_sizes = lax.optimization_barrier(jnp.sum(onehot, axis=-1))
    return unit_rows(summed / jnp.maximum(bead_sizes, 1.0)[..., None])

def kernel_slab(feats, beads, counts, types, point_unit, sparse_type):
    blocks = CONF // 16

    def one_block(items):
        block_feats, block_beads, block_counts, block_types = items
        units = bead_units(block_feats, block_beads)
        slots = jnp.arange(BEADS, dtype=jnp.int32)
        live_type = jnp.where(slots[None, :] < block_counts[:, None], block_types, -1)
        scores = jnp.dot(units.reshape(16 * BEADS, D), point_unit.T, preferred_element_type=jnp.float32)
        scores = (scores * D ** (-0.5)).reshape(16, BEADS, M)
        match = live_type[:, :, None] == sparse_type[None, None, :]
        values = jnp.where(match, jnp.exp(scores), jnp.zeros_like(scores))
        return lax.optimization_barrier(jnp.sum(values, axis=1)).astype(jnp.bfloat16)
    result = lax.map(one_block, (feats.reshape(blocks, 16, ATOMS, D), beads.reshape(blocks, 16, ATOMS), counts.reshape(blocks, 16), types.reshape(blocks, 16, BEADS)))
    return result.reshape(CONF, M)

def reference(atom_feats, atom_bead, bead_count, bead_type, sparse_points, sparse_type, targets):
    point_unit = unit_rows(sparse_points)
    kernels = []
    for slab_index in range(SLABS):
        kernels.append(kernel_slab(atom_feats[slab_index], atom_bead[slab_index], bead_count[slab_index], bead_type[slab_index], point_unit, sparse_type))
    kernel = jnp.concatenate(kernels, axis=0)
    gram = jnp.dot(kernel.T, kernel, preferred_element_type=jnp.float32) / TOTAL
    weights = jnp.transpose(targets, (1, 0, 2)).reshape(3, TOTAL)
    rhs = jnp.dot(weights, kernel.astype(jnp.float32), precision=lax.Precision.HIGHEST) / TOTAL
    return (gram.reshape(M, N_ROW, M // N_ROW), rhs)
```

```python
import jax
import jax.numpy as jnp
from jax import lax
from jax.sharding import PartitionSpec as P

EPSILON = 1e-06


def unit_rows(values):
    widened = values.astype(jnp.float32)
    scale = jnp.sqrt(jnp.mean(widened * widened, axis=-1, keepdims=True) + EPSILON)
    return (widened / scale).astype(jnp.bfloat16)


def bead_units(atom_feats, atom_bead, beads):
    slots = jnp.arange(beads, dtype=jnp.int32)
    onehot = (atom_bead[:, :, None, :] == slots[None, None, :, None]).astype(jnp.bfloat16)
    summed = jnp.einsum("sgba,sgad->sgbd", onehot, atom_feats, preferred_element_type=jnp.float32)
    bead_sizes = jnp.sum(onehot.astype(jnp.float32), axis=-1)
    return unit_rows(summed / jnp.maximum(bead_sizes, 1.0)[..., None])


def kernel_block(bead_unit, live_type, points, point_type):
    config_rows, beads, width = bead_unit.shape
    scores = jnp.einsum(
        "rd,md->rm",
        bead_unit.reshape(config_rows * beads, width),
        points,
        preferred_element_type=jnp.float32,
    )
    scores = (scores * width ** (-0.5)).reshape(config_rows, beads, points.shape[0])
    match = live_type[:, :, None] == point_type[None, None, :]
    values = jnp.where(match, jnp.exp(scores), jnp.zeros_like(scores))
    return jnp.sum(values, axis=1)


def shards(atom_feats, atom_bead, bead_count, bead_type, sparse_points, sparse_type, targets):
    slabs, local, atoms, width = atom_feats.shape
    beads = bead_type.shape[-1]
    config_rows = slabs * local
    units = bead_units(atom_feats, atom_bead, beads).reshape(config_rows, beads, width)
    slots = jnp.arange(beads, dtype=jnp.int32)
    live_type = jnp.where(slots[None, None, :] < bead_count[:, :, None], bead_type, -1).reshape(
        config_rows, beads
    )
    shard = sparse_points.shape[0]
    members = lax.axis_size("dp")
    rows = lax.axis_size("row")
    total = config_rows * members
    own = kernel_block(units, live_type, unit_rows(sparse_points), sparse_type).astype(jnp.bfloat16)
    columns = lax.all_gather(own, "dp", axis=0, tiled=True)
    weights = jnp.transpose(targets, (1, 0, 2)).reshape(3, config_rows)
    weights = lax.all_gather(weights, "dp", axis=1, tiled=True)
    rhs = jnp.dot(weights, columns.astype(jnp.float32), precision=lax.Precision.HIGHEST) / total
    width_rows = shard * lax.axis_size("col") // members
    strips_of = shard // width_rows
    member = lax.axis_index("dp")
    strip = lax.dynamic_slice_in_dim(columns, (member % strips_of) * width_rows, width_rows, 1)
    strips = lax.all_gather(strip, ("row", "col"), axis=0, tiled=False)
    strips = strips.reshape(rows, lax.axis_size("col"), total, width_rows)
    strips = lax.dynamic_index_in_dim(strips, member // strips_of, 1, keepdims=False)
    blocks = jnp.einsum("rni,nj->rij", strips, columns, preferred_element_type=jnp.float32)
    blocks = (blocks / total).astype(jnp.bfloat16)
    blocks = lax.all_to_all(blocks, "row", 0, 0, tiled=False)
    gram = jnp.transpose(blocks, (1, 0, 2)).astype(jnp.float32)
    return (gram, rhs)


def solution(mesh):
    return jax.shard_map(
        shards,
        mesh=mesh,
        in_specs=(
            P(None, "dp", None, None),
            P(None, "dp", None),
            P(None, "dp"),
            P(None, "dp", None),
            P(("row", "col"), None),
            P(("row", "col")),
            P(None, None, "dp"),
        ),
        out_specs=(P(("row", "dp"), None, "col"), P(None, ("row", "col"))),
        check_vma=False,
    )
```

```python
import functools

import jax
import jax.numpy as jnp
from jax import lax
from jax.experimental import pallas as pl
from jax.experimental.pallas import tpu as pltpu
from jax.sharding import PartitionSpec as P

EPSILON = 1e-06
MESH = pl.DeviceIdType.MESH
LOG2E = 1.4426950408889634

SIDE = 4
GROUP = 8
SUB = 32
HALF = 2 * SUB
STRIP = 128


def kernel(
    total,
    atoms_hbm, points_hbm, key_ref, live_ref, ptype_ref, weight_ref,
    gram_out, rhs_out,
    atoms, points, units, kbuf, sbuf, wbuf, acc, obuf,
    load_sem, k_send, k_recv, s_send, s_recv, w_send, w_recv, o_send, o_recv, o_local,
):
    width = points.shape[1]
    shard = points.shape[0]
    beads = units.shape[0] // SUB
    slots = beads * GROUP
    dp = lax.axis_index("dp")
    row = lax.axis_index("row")
    col = lax.axis_index("col")
    x, z = dp // SIDE, dp % SIDE
    h, core = row // 2, row % 2
    y = h * 2 + col
    at_strip = dp % 8
    owner = (dp // 8) == col

    def on_x(step):
        return {"dp": ((x + step) % SIDE) * SIDE + z, "row": row, "col": col}

    def on_z(step):
        return {"dp": x * SIDE + (z + step) % SIDE, "row": row, "col": col}

    def on_y(step, at_core):
        to = (y + step) % SIDE
        return {"dp": dp, "row": (to // 2) * 2 + at_core, "col": to % 2}

    sibling = on_y(0, 1 - core)
    up, down = on_y(1, core), on_y(-1, core)
    h_up, h_down = ((y + 1) % SIDE) // 2, ((y - 1) % SIDE) // 2

    loads = []
    order = (0, 2, 1, 3)
    per_sub = SUB // GROUP
    load_points = pltpu.make_async_copy(points_hbm, points, load_sem.at[4])
    load_points.start()
    for t in order:
        rows = pl.ds(t * per_sub, per_sub)
        copy = pltpu.make_async_copy(atoms_hbm.at[rows], atoms.at[rows], load_sem.at[t])
        copy.start()
        loads.append(copy)

    barrier = pltpu.get_barrier_semaphore()
    peers = [on_x(1), on_x(2), on_x(3), on_z(1), on_z(2), on_z(3), sibling, up, down]
    peers += [on_y(2, core), on_y(2, 1 - core)]
    for peer in peers:
        pl.semaphore_signal(barrier, inc=1, device_id=peer, device_id_type=MESH)

    wbuf[0, 0] = weight_ref[...]

    pending = []

    def remote(src, dst, send, recv, peer):
        return pltpu.make_async_remote_copy(
            src_ref=src, dst_ref=dst, send_sem=send, recv_sem=recv,
            device_id=peer, device_id_type=MESH,
        )

    def slot(route, outer, inner, sub):
        return kbuf.at[route, outer % SIDE, pl.ds((inner % SIDE) * HALF + sub * SUB, SUB), :]

    def recv_sem(route, outer, inner, sub):
        return k_recv.at[((route * SIDE + outer % SIDE) * SIDE + inner % SIDE) * 2 + sub]

    def along(route, phase, step):
        return on_x(step) if (route == 0) == (phase == 0) else on_z(step)

    def send(route, outer, inner, sub, phase, step):
        if phase == 0:
            to = (route, outer, inner - step, sub)
        else:
            to = (route, outer - step, inner, sub)
        copy = remote(
            slot(route, outer, inner, sub), slot(*to), k_send.at[len(pending)], recv_sem(*to),
            along(route, phase, step),
        )
        copy.start()
        pending.append(copy)

    def arrived(route, outer, inner, sub):
        here = slot(route, outer, inner, sub)
        remote(here, here, k_send.at[0], recv_sem(route, outer, inner, sub), sibling).wait_recv()

    def send_own(route, sub):
        for step in (1, -1):
            send(route, 0, 0, sub, 0, step)
        for step in (1, -1):
            send(route, 0, 0, sub, 1, step)

    def inner_step(route, inner, sub):
        arrived(route, 0, inner, sub)
        if inner == 3 and sub == 0:
            send(route, 0, inner, sub, 0, 1)
        if inner == 1 and sub == 1:
            send(route, 0, inner, sub, 0, -1)
        for step in (1, -1):
            send(route, 0, inner, sub, 1, step)

    def outer_step(route, inner):
        arrived(route, 3, inner, 0)
        send(route, 3, inner, 0, 1, 1)
        arrived(route, 1, inner, 1)
        send(route, 1, inner, 1, 1, -1)

    row_id = lax.broadcasted_iota(jnp.int32, (slots, GROUP * 32), 0)

    def unit_points():
        def body(i, carry):
            rows = pl.ds(pl.multiple_of(i * 128, 128), 128)
            wide = points[rows, :].astype(jnp.float32)
            mean = jnp.sum(wide * wide, axis=1, keepdims=True) * (1.0 / width)
            points[rows, :] = (wide * lax.rsqrt(mean + EPSILON)).astype(jnp.bfloat16)
            return carry
        lax.fori_loop(0, shard // 128, body, 0)

    def unit_beads(t):
        for i in range(per_sub):
            j = t * per_sub + i
            onehot = jnp.where(key_ref[j:j + 1, :] == row_id, 1.0, 0.0)
            size = jnp.maximum(jnp.sum(onehot, axis=1, keepdims=True), 1.0)
            summed = jnp.dot(onehot.astype(jnp.bfloat16), atoms[j], preferred_element_type=jnp.float32)
            inverse = 1.0 / size
            mean = jnp.sum(summed * summed, axis=1, keepdims=True) * (inverse * inverse * (1.0 / width))
            scale = inverse * lax.rsqrt(mean + EPSILON)
            units[i * slots:(i + 1) * slots, :] = (summed * scale).astype(jnp.bfloat16)

    def kernel_rows(t):
        route, sub = t // 2, t % 2
        tile = 256

        def body(ct, carry):
            cols = pl.ds(pl.multiple_of(ct * tile, tile), tile)
            scores = lax.dot_general(
                units[...], points[cols, :], (((1,), (1,)), ((), ())),
                preferred_element_type=jnp.float32,
            )
            kind = ptype_ref[:, cols]
            parts = []
            for i in range(per_sub):
                j = t * per_sub + i
                part = jnp.exp2(scores[i * slots:(i + 1) * slots] * (LOG2E * width ** (-0.5)))
                part = jnp.where(live_ref[:, j:j + 1] == kind, part, 0.0)
                parts.append(jnp.sum(part.reshape(beads, GROUP, tile), axis=0))
            kbuf[route, 0, sub * SUB:(sub + 1) * SUB, cols] = jnp.concatenate(parts, axis=0).astype(jnp.bfloat16)
            return carry
        lax.fori_loop(0, shard // tile, body, 0)

    groups = [(route, outer) for outer in (0, 3, 1, 2) for route in (0, 1)]
    index_of = {group: g for g, group in enumerate(groups)}

    def strip(g, r):
        return sbuf.at[g, pl.ds(pl.multiple_of(r * STRIP, STRIP), STRIP), :]

    def strip_copy(g, r, which, peer):
        here = strip(g, r)
        return remote(here, here, s_send.at[g * 4 + which], s_recv.at[g * 4 + r], peer)

    def strip_arrived(g, r):
        strip_copy(g, r, 0, sibling).wait_recv()

    def strip_send(group):
        g = index_of[group]

        @pl.when(owner)
        def _():
            route, outer = group
            lanes = pl.ds(pl.multiple_of(at_strip * STRIP, STRIP), STRIP)
            mine = kbuf[route, outer, :, lanes]
            sbuf[g, pl.ds(pl.multiple_of(row * STRIP, STRIP), STRIP), :] = mine.T
            strip_copy(g, row, 0, up).start()
            strip_copy(g, row, 1, down).start()
            strip_copy(g, row, 2, sibling).start()

    def strip_relay(group):
        g = index_of[group]
        other = (1 - h) * 2 + core
        r_up, r_down = h_up * 2 + core, h_down * 2 + core

        @pl.when(jnp.logical_not(owner))
        def _():
            strip_arrived(g, r_down)
            strip_copy(g, r_down, 0, sibling).start()
            strip_arrived(g, r_up)
            strip_copy(g, r_up, 1, sibling).start()

            @pl.when(h == g % 2)
            def _():
                strip_copy(g, r_down, 2, up).start()
                strip_copy(g, r_up, 3, down).start()

        @pl.when(owner)
        def _():
            strip_arrived(g, other)
            strip_copy(g, other, 3, sibling).start()

    def strip_drain(group):
        g = index_of[group]
        for which in range(2):
            strip_copy(g, row, which, sibling).wait_send()

        @pl.when(jnp.logical_or(owner, h == g % 2))
        def _():
            for which in range(2, 4):
                strip_copy(g, row, which, sibling).wait_send()

    def strips_here(group):
        g = index_of[group]
        strip_arrived(g, 1 - core)
        strip_arrived(g, 2 + 1 - core)

    def gram(group, first=False):
        g = index_of[group]
        strips_here(group)
        route, outer = group
        tile = 256

        def body(ct, carry):
            cols = pl.ds(pl.multiple_of(ct * tile, tile), tile)
            part = jnp.dot(sbuf[g], kbuf[route, outer, :, cols], preferred_element_type=jnp.float32)
            if first:
                acc[:, cols] = part
            else:
                acc[:, cols] += part
            return carry
        lax.fori_loop(0, shard // tile, body, 0)

    def weight_copy(axis, step):
        if axis == 0:
            src, dst, peer = wbuf.at[0, 0], wbuf.at[0, (-step) % SIDE], on_x(step)
        else:
            src, dst, peer = wbuf.at[0], wbuf.at[(-step) % SIDE], on_z(step)
        i = axis * 3 + step - 1
        return remote(src, dst, w_send.at[i], w_recv.at[i], peer)

    def weight_rows():
        low = lax.broadcasted_iota(jnp.int32, (8, 128), 1) < HALF
        for (route, outer), g in index_of.items():
            if route == 0:
                parts = [wbuf[outer, i] for i in range(SIDE)]
                pairs = [jnp.where(low, parts[i], pltpu.roll(parts[i + 1], HALF, 1)) for i in (0, 2)]
            else:
                parts = [wbuf[i, outer] for i in range(SIDE)]
                pairs = [jnp.where(low, pltpu.roll(parts[i], HALF, 1), parts[i + 1]) for i in (0, 2)]
            wide = jnp.concatenate(pairs, axis=1)
            high = wide.astype(jnp.bfloat16).astype(jnp.float32)
            both = jnp.concatenate([high, wide - high], axis=0)
            sbuf[g, 4 * STRIP:, :] = both.astype(jnp.bfloat16)

    load_points.wait()
    unit_points()
    loads[0].wait()
    unit_beads(0)
    kernel_rows(0)
    pl.semaphore_wait(barrier, len(peers))
    send_own(0, 0)
    for step in (1, 2, 3):
        weight_copy(0, step).start()
    loads[1].wait()
    unit_beads(2)
    kernel_rows(2)
    send_own(1, 0)
    loads[2].wait()
    unit_beads(1)
    kernel_rows(1)
    send_own(0, 1)
    inner_step(0, 3, 0)
    inner_step(0, 1, 0)
    for step in (1, 2, 3):
        weight_copy(0, step).wait_recv()
    for step in (1, 2, 3):
        weight_copy(1, step).start()
    loads[3].wait()
    unit_beads(3)
    kernel_rows(3)
    send_own(1, 1)
    inner_step(1, 3, 0)
    inner_step(1, 1, 0)
    for route in (0, 1):
        inner_step(route, 1, 1)
        inner_step(route, 3, 1)
    for route in (0, 1):
        outer_step(route, 0)
    for route in (0, 1):
        inner_step(route, 2, 0)
        inner_step(route, 2, 1)
    strip_send((0, 0))
    strip_send((1, 0))
    for route in (0, 1):
        outer_step(route, 3)
    for step in (1, 2, 3):
        weight_copy(1, step).wait_recv()
    weight_rows()
    strip_relay((0, 0))
    strip_relay((1, 0))
    for route in (0, 1):
        outer_step(route, 1)
    gram((0, 0), first=True)
    gram((1, 0))
    for route in (0, 1):
        outer_step(route, 2)
    for outer, sub in ((3, 1), (1, 0)):
        for route in (0, 1):
            for inner in range(SIDE):
                arrived(route, outer, inner, sub)
            strip_send((route, outer))
    for outer in (3, 1):
        for route in (0, 1):
            strip_relay((route, outer))
    for outer in (3, 1):
        for route in (0, 1):
            gram((route, outer))
    for route in (0, 1):
        for inner in (0, 3, 1, 2):
            for sub in (0, 1):
                arrived(route, 2, inner, sub)
        strip_send((route, 2))
    for route in (0, 1):
        strip_relay((route, 2))
    for route in (0, 1):
        strips_here((route, 2))

    def finish(rows, cols):
        value = acc[rows, cols]
        for route in (0, 1):
            g = index_of[(route, 2)]
            value += jnp.dot(sbuf[g, rows, :], kbuf[route, 2, :, cols], preferred_element_type=jnp.float32)
        return value * (1.0 / total)

    def block(r):
        rows = pl.ds(pl.multiple_of(r * STRIP, STRIP), STRIP)
        obuf[r] = finish(rows, pl.ds(0, shard)).astype(jnp.bfloat16)

    def out_copy(r, which, peer):
        return remote(obuf.at[r], gram_out.at[row], o_send.at[which], o_recv.at[r], peer)

    far = (1 - h) * 2
    targets = [
        (far + core, on_y(2, core)), (far + 1 - core, on_y(2, 1 - core)), (h * 2 + 1 - core, sibling),
    ]
    for which, (r, peer) in enumerate(targets):
        block(r)
        remote(obuf.at[r], gram_out.at[row], o_send.at[which], o_recv.at[row], peer).start()
    block(row)
    keep = pltpu.make_async_copy(obuf.at[row], gram_out.at[row], o_local)
    keep.start()
    tail = finish(pl.ds(4 * STRIP, 16), pl.ds(0, shard))
    rhs_out[...] = tail[0:3] + tail[8:11]
    for copy in pending:
        copy.wait_send()
    for group in groups:
        strip_drain(group)
    for axis in (0, 1):
        for step in (1, 2, 3):
            weight_copy(axis, step).wait_send()
    keep.wait()
    for which, (r, peer) in enumerate(targets):
        copy = remote(obuf.at[r], gram_out.at[r], o_send.at[which], o_recv.at[r], peer)
        copy.wait_send()
        copy.wait_recv()


def shards(atom_feats, atom_bead, bead_count, bead_type, sparse_points, sparse_type, targets):
    slabs, local, atoms, width = atom_feats.shape
    beads = bead_type.shape[-1]
    config_rows = slabs * local
    shard = sparse_points.shape[0]
    total = config_rows * lax.axis_size("dp")
    blocks = config_rows // GROUP
    place = jnp.arange(GROUP * atoms, dtype=jnp.int32)[None, :] // atoms
    key = atom_bead.reshape(blocks, GROUP * atoms) * GROUP + place
    slots = jnp.arange(beads, dtype=jnp.int32)
    live = jnp.where(slots[None, None, :] < bead_count[:, :, None], bead_type, -1)
    live = jnp.transpose(live.reshape(blocks, GROUP, beads), (2, 1, 0)).reshape(beads * GROUP, blocks)
    weights = jnp.transpose(targets, (1, 0, 2)).reshape(3, config_rows)
    weights = jnp.pad(weights, ((0, 5), (0, 0)))
    bf16, f32 = jnp.bfloat16, jnp.float32
    dma = pltpu.SemaphoreType.DMA
    vmem = pl.BlockSpec(memory_space=pltpu.VMEM)
    hbm = pl.BlockSpec(memory_space=pl.ANY)
    gram, rhs = pl.pallas_call(
        functools.partial(kernel, total),
        out_shape=(
            jax.ShapeDtypeStruct((4, STRIP, shard), bf16),
            jax.ShapeDtypeStruct((3, shard), f32),
        ),
        in_specs=[hbm, hbm, vmem, vmem, vmem, vmem],
        out_specs=(hbm, vmem),
        scratch_shapes=[
            pltpu.VMEM((blocks, GROUP * atoms, width), bf16),
            pltpu.VMEM((shard, width), bf16),
            pltpu.VMEM((SUB * beads, width), bf16),
            pltpu.VMEM((2, SIDE, SIDE * HALF, shard), bf16),
            pltpu.VMEM((8, 4 * STRIP + 16, SIDE * HALF), bf16),
            pltpu.VMEM((SIDE, SIDE, 8, 128), f32),
            pltpu.VMEM((4 * STRIP + 16, shard), f32),
            pltpu.VMEM((4, STRIP, shard), bf16),
            dma((5,)),
            dma((60,)),
            dma((64,)),
            dma((32,)),
            dma((32,)),
            dma((6,)),
            dma((6,)),
            dma((3,)),
            dma((4,)),
            dma,
        ],
        compiler_params=pltpu.CompilerParams(
            collective_id=0, has_side_effects=True, vmem_limit_bytes=44 * 1024 * 1024
        ),
    )(
        atom_feats.reshape(blocks, GROUP * atoms, width), sparse_points, key, live,
        sparse_type.reshape(1, shard), weights,
    )
    return (jnp.transpose(gram, (1, 0, 2)).astype(jnp.float32), rhs)


def solution(mesh):
    return jax.shard_map(
        shards,
        mesh=mesh,
        in_specs=(
            P(None, "dp", None, None),
            P(None, "dp", None),
            P(None, "dp"),
            P(None, "dp", None),
            P(("row", "col"), None),
            P(("row", "col")),
            P(None, None, "dp"),
        ),
        out_specs=(P(("row", "dp"), None, "col"), P(None, ("row", "col"))),
        check_vma=False,
    )
```

```python
import functools

import jax
import jax.numpy as jnp
from jax import lax
from jax.experimental import pallas as pl
from jax.experimental.pallas import tpu as pltpu
from jax.sharding import PartitionSpec as P

EPSILON = 1e-06
MESH = pl.DeviceIdType.MESH
LOG2E = 1.4426950408889634

SIDE = 4
GROUP = 8
SUB = 32
HALF = 2 * SUB
STRIP = 128
ATOMS = 32
BEADS = 16


def kernel(
    total,
    atoms_hbm, points_hbm, bead_hbm, count_hbm, type_hbm, ptype_hbm, targets_hbm,
    gram_out, rhs_out,
    atoms, points, units, kbuf, rbuf, sbuf, wbuf, acc, obuf,
    bead_in, count_in, type_in, ptype, targets_in, repeated, live,
    load_sem, k_send, k_recv, d_send, d_recv, s_send, s_recv, w_send, w_recv, o_send, o_recv, o_local,
):
    width = points.shape[1]
    shard = points.shape[0]
    slots = BEADS * GROUP
    dp = lax.axis_index("dp")
    row = lax.axis_index("row")
    col = lax.axis_index("col")
    x, z = dp // SIDE, dp % SIDE
    h, core = row // 2, row % 2
    y = h * 2 + col
    at_strip = dp % 8
    owner = (dp // 8) == col

    def on_plane(step_x, step_z):
        return {"dp": ((x + step_x) % SIDE) * SIDE + (z + step_z) % SIDE, "row": row, "col": col}

    def on_x(step):
        return on_plane(step, 0)

    def on_z(step):
        return on_plane(0, step)

    def on_y(step, at_core):
        to = (y + step) % SIDE
        return {"dp": dp, "row": (to // 2) * 2 + at_core, "col": to % 2}

    sibling = on_y(0, 1 - core)
    up, down = on_y(1, core), on_y(-1, core)
    h_up, h_down = ((y + 1) % SIDE) // 2, ((y - 1) % SIDE) // 2
    offsets = [(i, j) for i in range(SIDE) for j in range(SIDE) if (i, j) != (0, 0)]

    loads = []
    compute_order = order = (0, 2, 1, 3)
    per_sub = SUB // GROUP
    small = []
    for i, (src, dst) in enumerate((
        (bead_hbm, bead_in), (count_hbm, count_in), (type_hbm, type_in), (ptype_hbm, ptype),
        (targets_hbm, targets_in),
    )):
        copy = pltpu.make_async_copy(src, dst, load_sem.at[5 + i])
        copy.start()
        small.append(copy)
    load_points = pltpu.make_async_copy(points_hbm, points, load_sem.at[4])
    load_points.start()
    for t in order:
        rows = pl.ds(t * per_sub, per_sub)
        copy = pltpu.make_async_copy(atoms_hbm.at[rows], atoms.at[rows], load_sem.at[t])
        copy.start()
        loads.append(copy)

    barrier = pltpu.get_barrier_semaphore()
    peers = [on_plane(*offset) for offset in offsets]
    peers += [sibling, up, down, on_y(2, core), on_y(2, 1 - core)]
    for peer in peers:
        pl.semaphore_signal(barrier, inc=1, device_id=peer, device_id_type=MESH)

    pending = []

    def remote(src, dst, send, recv, peer):
        return pltpu.make_async_remote_copy(
            src_ref=src, dst_ref=dst, send_sem=send, recv_sem=recv,
            device_id=peer, device_id_type=MESH,
        )

    def slot(route, outer, inner, sub):
        return kbuf.at[route, outer % SIDE, pl.ds((inner % SIDE) * HALF + sub * SUB, SUB), :]

    def recv_sem(route, outer, inner, sub):
        return k_recv.at[((route * SIDE + outer % SIDE) * SIDE + inner % SIDE) * 2 + sub]

    def along(route, phase, step):
        return on_x(step) if (route == 0) == (phase == 0) else on_z(step)

    def send(route, outer, inner, sub, phase, step):
        if phase == 0:
            to = (route, outer, inner - step, sub)
        else:
            to = (route, outer - step, inner, sub)
        copy = remote(
            slot(route, outer, inner, sub), slot(*to), k_send.at[len(pending)], recv_sem(*to),
            along(route, phase, step),
        )
        copy.start()
        pending.append(copy)

    def arrived(route, outer, inner, sub):
        here = slot(route, outer, inner, sub)
        remote(here, here, k_send.at[0], recv_sem(route, outer, inner, sub), sibling).wait_recv()

    def send_own(route, sub):
        for step in (1, -1):
            send(route, 0, 0, sub, 0, step)
        for step in (1, -1):
            send(route, 0, 0, sub, 1, step)

    def inner_step(route, inner, sub):
        arrived(route, 0, inner, sub)
        if inner == 3 and sub == 0:
            send(route, 0, inner, sub, 0, 1)
        if inner == 1 and sub == 1:
            send(route, 0, inner, sub, 0, -1)
        for step in (1, -1):
            send(route, 0, inner, sub, 1, step)

    def outer_step(route, inner, sub):
        if sub == 0:
            arrived(route, 3, inner, 0)
            send(route, 3, inner, 0, 1, 1)
        else:
            arrived(route, 1, inner, 1)
            send(route, 1, inner, 1, 1, -1)

    def near(route, sub):
        for inner in (3, 1) if sub == 0 else (1, 3):
            inner_step(route, inner, sub)
        outer_step(route, 0, sub)

    def middle(route, sub):
        inner_step(route, 2, sub)
        outer_step(route, 3, sub)
        outer_step(route, 1, sub)

    def far(route, sub):
        outer_step(route, 2, sub)

    def prepare():
        for copy in small:
            copy.wait()
        wbuf[0, 0] = jnp.zeros_like(wbuf[0, 0])
        wbuf[0, 0, 0:3, :] = jnp.concatenate([targets_in[:, 0], targets_in[:, 1]], axis=1)
        spread = lax.broadcasted_iota(jnp.int32, (ATOMS, 128), 1) % ATOMS
        spread = jnp.where(spread == lax.broadcasted_iota(jnp.int32, (ATOMS, 128), 0), 1.0, 0.0)
        for s in range(2):
            here = slice(s * HALF, (s + 1) * HALF)
            beads = bead_in[s].astype(jnp.float32).astype(jnp.bfloat16)
            repeated[here, :] = lax.dot_general(
                beads, spread.astype(jnp.bfloat16), (((0,), (0,)), ((), ())), preferred_element_type=jnp.float32
            )
            alive = lax.broadcasted_iota(jnp.int32, (BEADS, HALF), 0) < count_in[s:s + 1, :]
            kinds = jnp.where(alive, type_in[s], -1).astype(jnp.float32).astype(jnp.bfloat16)
            same = lax.broadcasted_iota(jnp.int32, (BEADS, BEADS), 0)
            same = same == lax.broadcasted_iota(jnp.int32, (BEADS, BEADS), 1)
            kinds = lax.dot_general(
                kinds, jnp.where(same, 1.0, 0.0).astype(jnp.bfloat16), (((0,), (0,)), ((), ())),
                preferred_element_type=jnp.float32,
            )
            for i in range(HALF // GROUP):
                rows = kinds[i * GROUP:(i + 1) * GROUP]
                for b in range(BEADS):
                    live[s * (HALF // GROUP) + i, b * GROUP:(b + 1) * GROUP, :] = jnp.broadcast_to(
                        rows[:, b:b + 1], (GROUP, 128)
                    )

    bead_id = (lax.broadcasted_iota(jnp.int32, (slots, GROUP * ATOMS), 0) // GROUP).astype(jnp.float32)
    member = lax.broadcasted_iota(jnp.int32, (GROUP, GROUP * ATOMS), 1) // ATOMS
    member = member == lax.broadcasted_iota(jnp.int32, (GROUP, GROUP * ATOMS), 0)

    def unit_points():
        def body(i, carry):
            rows = pl.ds(pl.multiple_of(i * 128, 128), 128)
            wide = points[rows, :].astype(jnp.float32)
            mean = jnp.sum(wide * wide, axis=1, keepdims=True) * (1.0 / width)
            points[rows, :] = (wide * lax.rsqrt(mean + EPSILON)).astype(jnp.bfloat16)
            return carry
        lax.fori_loop(0, shard // 128, body, 0)

    def unit_beads(t):
        for i in range(per_sub):
            j = t * per_sub + i
            near_atoms = repeated[j * GROUP:(j + 1) * GROUP, :]
            own = jnp.where(member, jnp.concatenate([near_atoms, near_atoms], axis=1), -1.0)
            onehot = jnp.where(jnp.concatenate([own] * BEADS, axis=0) == bead_id, 1.0, 0.0)
            size = jnp.maximum(jnp.sum(onehot, axis=1, keepdims=True), 1.0)
            summed = jnp.dot(onehot.astype(jnp.bfloat16), atoms[j], preferred_element_type=jnp.float32)
            inverse = 1.0 / size
            mean = jnp.sum(summed * summed, axis=1, keepdims=True) * (inverse * inverse * (1.0 / width))
            scale = inverse * lax.rsqrt(mean + EPSILON)
            units[compute_order.index(t) % 2, i * slots:(i + 1) * slots, :] = (summed * scale).astype(jnp.bfloat16)

    def kernel_rows(t):
        route, sub = t // 2, t % 2
        tile = 256
        for cols in (slice(i, i + tile) for i in range(0, shard, tile)):
            scores = lax.dot_general(
                units[compute_order.index(t) % 2], points[cols, :], (((1,), (1,)), ((), ())), preferred_element_type=jnp.float32,
            )
            kind = ptype[:, cols].astype(jnp.float32)
            parts = []
            for i in range(per_sub):
                j = t * per_sub + i
                part = jnp.exp2(scores[i * slots:(i + 1) * slots] * (LOG2E * width ** (-0.5)))
                alive = live[j]
                part = jnp.where(jnp.concatenate([alive] * (tile // 128), axis=1) == kind, part, 0.0)
                parts.append(jnp.sum(part.reshape(BEADS, GROUP, tile), axis=0))
            kbuf[route, 0, sub * SUB:(sub + 1) * SUB, cols] = jnp.concatenate(parts, axis=0).astype(jnp.bfloat16)

    groups = [(route, outer) for outer in (0, 3, 1, 2) for route in (0, 1)]
    index_of = {group: g for g, group in enumerate(groups)}

    def relative(route, step_x, step_z):
        return (step_z % SIDE, step_x % SIDE) if route == 0 else (step_x % SIDE, step_z % SIDE)

    def direct(route, n, to_x, to_z, s):
        outer, inner = relative(route, -to_x, -to_z)
        lanes = pl.ds(pl.multiple_of(s * STRIP, STRIP), STRIP)
        return remote(
            kbuf.at[route, 0, pl.ds(0, HALF), lanes],
            rbuf.at[route, outer, pl.ds(inner * HALF, HALF), :],
            d_send.at[route * 15 + n],
            d_recv.at[(route * SIDE + outer) * SIDE + inner],
            on_plane(to_x, to_z),
        )

    def direct_each(route, do):
        for n, (to_x, to_z) in enumerate(offsets):
            there_x, there_z = (x + to_x) % SIDE, (z + to_z) % SIDE

            @pl.when(there_x // 2 == col)
            def _():
                do(direct(route, n, to_x, to_z, (there_x % 2) * SIDE + there_z))

    def strip(g, r):
        return sbuf.at[g, pl.ds(pl.multiple_of(r * STRIP, STRIP), STRIP), :]

    def strip_copy(g, r, which, peer):
        here = strip(g, r)
        return remote(here, here, s_send.at[g * 4 + which], s_recv.at[g * 4 + r], peer)

    def strip_arrived(g, r):
        strip_copy(g, r, 0, sibling).wait_recv()

    def strip_send(group):
        g = index_of[group]
        route, outer = group

        @pl.when(owner)
        def _():
            for inner in range(SIDE):
                if (outer, inner) == (0, 0):
                    lanes = pl.ds(pl.multiple_of(at_strip * STRIP, STRIP), STRIP)
                    rbuf[route, 0, 0:HALF, :] = kbuf[route, 0, 0:HALF, lanes]
                else:
                    here = rbuf.at[route, outer, pl.ds(inner * HALF, HALF), :]
                    remote(
                        here, here, d_send.at[0], d_recv.at[(route * SIDE + outer) * SIDE + inner], sibling
                    ).wait_recv()
            sbuf[g, pl.ds(pl.multiple_of(row * STRIP, STRIP), STRIP), :] = rbuf[route, outer].T
            strip_copy(g, row, 0, up).start()
            strip_copy(g, row, 1, down).start()
            strip_copy(g, row, 2, sibling).start()

    def strip_relay(group):
        g = index_of[group]
        r_up, r_down = h_up * 2 + core, h_down * 2 + core

        @pl.when(jnp.logical_not(owner))
        def _():
            strip_arrived(g, r_down)
            strip_arrived(g, r_up)

            @pl.when(h == (g // 2) % 2)
            def _():
                strip_copy(g, r_down, 2, up).start()
                strip_copy(g, r_up, 3, down).start()
            strip_copy(g, r_down, 0, sibling).start()
            strip_copy(g, r_up, 1, sibling).start()

    def strip_last(group):
        g = index_of[group]
        other = (1 - h) * 2 + core

        @pl.when(owner)
        def _():
            strip_arrived(g, other)
            strip_copy(g, other, 3, sibling).start()

    def strip_drain(group):
        g = index_of[group]
        for which in range(2):
            strip_copy(g, row, which, sibling).wait_send()

        @pl.when(jnp.logical_or(owner, h == (g // 2) % 2))
        def _():
            for which in range(2, 4):
                strip_copy(g, row, which, sibling).wait_send()

    def strips_here(group):
        g = index_of[group]
        strip_arrived(g, 1 - core)
        strip_arrived(g, 2 + 1 - core)

    def gram(group, first=False):
        g = index_of[group]
        strips_here(group)
        route, outer = group
        tile = 256

        def body(ct, carry):
            cols = pl.ds(pl.multiple_of(ct * tile, tile), tile)
            part = jnp.dot(sbuf[g], kbuf[route, outer, :, cols], preferred_element_type=jnp.float32)
            if first:
                acc[:, cols] = part
            else:
                acc[:, cols] += part
            return carry
        lax.fori_loop(0, shard // tile, body, 0)

    def weight_copy(axis, step):
        if axis == 0:
            src, dst, peer = wbuf.at[0, 0], wbuf.at[0, (-step) % SIDE], on_x(step)
        else:
            src, dst, peer = wbuf.at[0], wbuf.at[(-step) % SIDE], on_z(step)
        i = axis * 3 + step - 1
        return remote(src, dst, w_send.at[i], w_recv.at[i], peer)

    def weight_rows():
        low = lax.broadcasted_iota(jnp.int32, (8, 128), 1) < HALF
        for (route, outer), g in index_of.items():
            if route == 0:
                parts = [wbuf[outer, i] for i in range(SIDE)]
                pairs = [jnp.where(low, parts[i], pltpu.roll(parts[i + 1], HALF, 1)) for i in (0, 2)]
            else:
                parts = [wbuf[i, outer] for i in range(SIDE)]
                pairs = [jnp.where(low, pltpu.roll(parts[i], HALF, 1), parts[i + 1]) for i in (0, 2)]
            wide = jnp.concatenate(pairs, axis=1)
            high = wide.astype(jnp.bfloat16).astype(jnp.float32)
            both = jnp.concatenate([high, wide - high], axis=0)
            sbuf[g, 4 * STRIP:, :] = both.astype(jnp.bfloat16)

    prepare()
    load_points.wait()
    unit_points()
    loads[0].wait()
    unit_beads(0)

    def compute(n):
        if n + 1 < 4:
            loads[n + 1].wait()
            unit_beads(compute_order[n + 1])
        kernel_rows(compute_order[n])

    def gather_rest(route, outer):
        for inner in (0, 3, 1, 2):
            for sub in {0: (), 3: (1,), 1: (0,), 2: (0, 1)}[outer]:
                arrived(route, outer, inner, sub)

    for n in range(3):
        compute(n)
    pl.semaphore_wait(barrier, len(peers))
    direct_each(0, lambda copy: copy.start())
    for step in (1, 2, 3):
        weight_copy(0, step).start()
    send_own(1, 0)
    send_own(0, 0)
    compute(3)
    direct_each(1, lambda copy: copy.start())
    send_own(1, 1)
    strip_send((0, 1))
    strip_send((0, 0))
    send_own(0, 1)
    near(1, 0)
    strip_send((0, 3))
    near(0, 0)
    strip_send((0, 2))
    strip_send((1, 0))
    near(0, 1)
    strip_send((1, 2))
    strip_send((1, 3))
    strip_relay((0, 3))
    strip_relay((0, 0))
    strip_send((1, 1))
    strip_relay((0, 1))
    near(1, 1)
    for step in (1, 2, 3):
        weight_copy(0, step).wait_recv()
    for step in (1, 2, 3):
        weight_copy(1, step).start()
    strip_relay((0, 2))
    middle(1, 0)
    strip_relay((1, 0))
    middle(0, 0)
    middle(0, 1)
    strip_last((0, 2))
    strip_relay((1, 2))
    strip_last((0, 0))
    strip_relay((1, 3))
    strip_relay((1, 1))
    strip_last((1, 0))
    middle(1, 1)
    for step in (1, 2, 3):
        weight_copy(1, step).wait_recv()
    weight_rows()
    gather_rest(0, 0)
    gram((0, 0), first=True)
    strip_last((0, 1))
    gather_rest(1, 0)
    gram((1, 0))
    strip_last((0, 3))
    far(0, 0)
    far(0, 1)
    strip_last((1, 3))
    strip_last((1, 1))
    far(1, 0)
    strip_last((1, 2))
    gather_rest(0, 1)
    gram((0, 1))
    far(1, 1)
    gather_rest(1, 1)
    gram((1, 1))
    gather_rest(1, 3)
    gram((1, 3))
    gather_rest(0, 3)
    gram((0, 3))
    for route in (0, 1):
        gather_rest(route, 2)
        strips_here((route, 2))

    def finish(rows, cols):
        value = acc[rows, cols]
        for route in (0, 1):
            g = index_of[(route, 2)]
            value += jnp.dot(sbuf[g, rows, :], kbuf[route, 2, :, cols], preferred_element_type=jnp.float32)
        return value * (1.0 / total)

    def block(r):
        rows = pl.ds(pl.multiple_of(r * STRIP, STRIP), STRIP)
        obuf[r] = finish(rows, pl.ds(0, shard)).astype(jnp.bfloat16)

    across = (1 - h) * 2
    targets = [
        (across + core, on_y(2, core)), (across + 1 - core, on_y(2, 1 - core)), (h * 2 + 1 - core, sibling),
    ]
    for which, (r, peer) in enumerate(targets):
        block(r)
        remote(obuf.at[r], gram_out.at[row], o_send.at[which], o_recv.at[row], peer).start()
    block(row)
    keep = pltpu.make_async_copy(obuf.at[row], gram_out.at[row], o_local)
    keep.start()
    tail = finish(pl.ds(4 * STRIP, 16), pl.ds(0, shard))
    rhs_out[...] = tail[0:8] + tail[8:16]
    for copy in pending:
        copy.wait_send()
    for route in (0, 1):
        direct_each(route, lambda copy: copy.wait_send())
    for group in groups:
        strip_drain(group)
    for axis in (0, 1):
        for step in (1, 2, 3):
            weight_copy(axis, step).wait_send()
    keep.wait()
    for which, (r, peer) in enumerate(targets):
        copy = remote(obuf.at[r], gram_out.at[r], o_send.at[which], o_recv.at[r], peer)
        copy.wait_send()
        copy.wait_recv()


def widen(gram_in, rhs_in, gram_out, rhs_out):
    for q in range(4):
        gram_out[:, q, :] = gram_in[q].astype(jnp.float32)
    rhs_out[...] = rhs_in[0:3, :]


def shards(atom_feats, atom_bead, bead_count, bead_type, sparse_points, sparse_type, targets):
    slabs, local, atoms, width = atom_feats.shape
    config_rows = slabs * local
    shard = sparse_points.shape[0]
    total = config_rows * lax.axis_size("dp")
    blocks = config_rows // GROUP
    bf16, f32, i32 = jnp.bfloat16, jnp.float32, jnp.int32
    dma = pltpu.SemaphoreType.DMA
    vmem = pl.BlockSpec(memory_space=pltpu.VMEM)
    hbm = pl.BlockSpec(memory_space=pltpu.HBM)
    gram, rhs = pl.pallas_call(
        functools.partial(kernel, total),
        out_shape=(
            jax.ShapeDtypeStruct((4, STRIP, shard), bf16),
            jax.ShapeDtypeStruct((8, shard), f32),
        ),
        in_specs=[hbm] * 7,
        out_specs=(hbm, vmem),
        scratch_shapes=[
            pltpu.VMEM((blocks, GROUP * atoms, width), bf16),
            pltpu.VMEM((shard, width), bf16),
            pltpu.VMEM((2, SUB * BEADS, width), bf16),
            pltpu.VMEM((2, SIDE, SIDE * HALF, shard), bf16),
            pltpu.VMEM((2, SIDE, SIDE * HALF, STRIP), bf16),
            pltpu.VMEM((8, 4 * STRIP + 16, SIDE * HALF), bf16),
            pltpu.VMEM((SIDE, SIDE, 8, 128), f32),
            pltpu.VMEM((4 * STRIP + 16, shard), f32),
            pltpu.VMEM((4, STRIP, shard), bf16),
            pltpu.VMEM((slabs, atoms, local), i32),
            pltpu.VMEM(bead_count.shape, i32),
            pltpu.VMEM((slabs, BEADS, local), i32),
            pltpu.VMEM((1, shard), i32),
            pltpu.VMEM((3, slabs, local), f32),
            pltpu.VMEM((config_rows, 128), f32),
            pltpu.VMEM((blocks, BEADS * GROUP, 128), f32),
            dma((10,)),
            dma((60,)),
            dma((64,)),
            dma((30,)),
            dma((32,)),
            dma((32,)),
            dma((32,)),
            dma((6,)),
            dma((6,)),
            dma((3,)),
            dma((4,)),
            dma,
        ],
        compiler_params=pltpu.CompilerParams(
            collective_id=0, has_side_effects=True, vmem_limit_bytes=60 * 1024 * 1024
        ),
    )(
        atom_feats.reshape(blocks, GROUP * atoms, width), sparse_points, jnp.swapaxes(atom_bead, 1, 2),
        bead_count, jnp.swapaxes(bead_type, 1, 2), sparse_type.reshape(1, shard), jnp.swapaxes(targets, 0, 1),
    )
    steps = 2
    return pl.pallas_call(
        widen,
        grid=(steps,),
        out_shape=(
            jax.ShapeDtypeStruct((STRIP, 4, shard), f32),
            jax.ShapeDtypeStruct((3, shard), f32),
        ),
        in_specs=[
            pl.BlockSpec((4, STRIP // steps, shard), lambda i: (0, i, 0)),
            pl.BlockSpec((8, shard), lambda i: (0, 0)),
        ],
        out_specs=(
            pl.BlockSpec((STRIP // steps, 4, shard), lambda i: (i, 0, 0)),
            pl.BlockSpec((3, shard), lambda i: (0, 0)),
        ),
        compiler_params=pltpu.CompilerParams(vmem_limit_bytes=60 * 1024 * 1024),
    )(gram, rhs)


def solution(mesh):
    return jax.shard_map(
        shards,
        mesh=mesh,
        in_specs=(
            P(None, "dp", None, None),
            P(None, "dp", None),
            P(None, "dp"),
            P(None, "dp", None),
            P(("row", "col"), None),
            P(("row", "col")),
            P(None, None, "dp"),
        ),
        out_specs=(P(("row", "dp"), None, "col"), P(None, ("row", "col"))),
        check_vma=False,
    )
```

```python
import functools

import jax
import jax.numpy as jnp
from jax import lax
from jax.experimental import pallas as pl
from jax.experimental.pallas import tpu as pltpu
from jax.sharding import PartitionSpec as P

EPSILON = 1e-06
MESH = pl.DeviceIdType.MESH
LOG2E = 1.4426950408889634

SIDE = 4
GROUP = 8
SUB = 32
HALF = 2 * SUB
STRIP = 128
ATOMS = 32
BEADS = 16
RELAYED = ((0, 32), (32, 16))
DIRECT = 48
TURNS = (-1, 1)


def kernel(
    total,
    atoms_hbm, points_hbm, bead_hbm, count_hbm, type_hbm, ptype_hbm, targets_hbm,
    gram_out, rhs_out,
    atoms, points, units, kbuf, rbuf, sbuf, wbuf, acc, obuf, tbuf, relay,
    bead_in, count_in, type_in, ptype, targets_in, repeated, live,
    load_sem, k_send, k_recv, d_send, d_recv, s_send, s_recv, w_send, w_recv, o_send, o_recv, o_local, t_send, t_recv, y_send, y_recv, f_send, f_recv,
):
    width = points.shape[1]
    shard = points.shape[0]
    slots = BEADS * GROUP
    dp = lax.axis_index("dp")
    row = lax.axis_index("row")
    col = lax.axis_index("col")
    x, z = dp // SIDE, dp % SIDE
    h, core = row // 2, row % 2
    y = h * 2 + col
    at_strip = dp % 8
    owner = (dp // 8) == col

    def on_plane(step_x, step_z):
        return {"dp": ((x + step_x) % SIDE) * SIDE + (z + step_z) % SIDE, "row": row, "col": col}

    def on_x(step):
        return on_plane(step, 0)

    def on_z(step):
        return on_plane(0, step)

    def on_y(step, at_core):
        to = (y + step) % SIDE
        return {"dp": dp, "row": (to // 2) * 2 + at_core, "col": to % 2}

    sibling = on_y(0, 1 - core)
    up, down = on_y(1, core), on_y(-1, core)
    h_up, h_down = ((y + 1) % SIDE) // 2, ((y - 1) % SIDE) // 2
    offsets = [(i, j) for i in range(SIDE) for j in range(SIDE) if (i, j) != (0, 0)]

    loads = []
    compute_order = order = (0, 1, 2, 3)
    per_sub = SUB // GROUP
    small = []
    for i, (src, dst) in enumerate((
        (bead_hbm, bead_in), (count_hbm, count_in), (type_hbm, type_in), (ptype_hbm, ptype),
        (targets_hbm, targets_in),
    )):
        copy = pltpu.make_async_copy(src, dst, load_sem.at[5 + i])
        copy.start()
        small.append(copy)
    load_points = pltpu.make_async_copy(points_hbm, points, load_sem.at[4])
    load_points.start()
    for t in order:
        rows = pl.ds(t * per_sub, per_sub)
        copy = pltpu.make_async_copy(atoms_hbm.at[rows], atoms.at[rows], load_sem.at[t])
        copy.start()
        loads.append(copy)

    barrier = pltpu.get_barrier_semaphore()
    peers = [on_plane(*offset) for offset in offsets]
    peers += [sibling, up, down, on_y(2, core), on_y(2, 1 - core)]
    for peer in peers:
        pl.semaphore_signal(barrier, inc=1, device_id=peer, device_id_type=MESH)

    pending = []

    def remote(src, dst, send, recv, peer):
        return pltpu.make_async_remote_copy(
            src_ref=src, dst_ref=dst, send_sem=send, recv_sem=recv,
            device_id=peer, device_id_type=MESH,
        )

    def slot(route, outer, inner, sub):
        return kbuf.at[route, outer % SIDE, pl.ds((inner % SIDE) * HALF + sub * SUB, SUB), :]

    def recv_sem(route, outer, inner, sub):
        return k_recv.at[((route * SIDE + outer % SIDE) * SIDE + inner % SIDE) * 2 + sub]

    def along(route, phase, step):
        return on_x(step) if (route == 0) == (phase == 0) else on_z(step)

    def send(route, outer, inner, sub, phase, step):
        if phase == 0:
            to = (route, outer, inner - step, sub)
        else:
            to = (route, outer - step, inner, sub)
        copy = remote(
            slot(route, outer, inner, sub), slot(*to), k_send.at[len(pending)], recv_sem(*to),
            along(route, phase, step),
        )
        copy.start()
        pending.append(copy)

    def arrived(route, outer, inner, sub):
        here = slot(route, outer, inner, sub)
        remote(here, here, k_send.at[0], recv_sem(route, outer, inner, sub), sibling).wait_recv()

    def send_own(route, sub):
        for step in (1, -1):
            send(route, 0, 0, sub, 0, step)
        for step in (1, -1):
            send(route, 0, 0, sub, 1, step)

    def inner_step(route, inner, sub):
        arrived(route, 0, inner, sub)
        if inner == 3 and sub == 0:
            send(route, 0, inner, sub, 0, 1)
        if inner == 1 and sub == 1:
            send(route, 0, inner, sub, 0, -1)
        for step in (1, -1):
            send(route, 0, inner, sub, 1, step)

    def outer_step(route, inner, sub):
        if sub == 0:
            arrived(route, 3, inner, 0)
            send(route, 3, inner, 0, 1, 1)
        else:
            arrived(route, 1, inner, 1)
            send(route, 1, inner, 1, 1, -1)

    def near(route, sub):
        for inner in (3, 1) if sub == 0 else (1, 3):
            inner_step(route, inner, sub)
        outer_step(route, 0, sub)

    def middle(route, sub):
        inner_step(route, 2, sub)
        outer_step(route, 3, sub)
        outer_step(route, 1, sub)

    def far(route, sub):
        outer_step(route, 2, sub)

    def prepare():
        for copy in small:
            copy.wait()
        wbuf[0, 0] = jnp.zeros_like(wbuf[0, 0])
        wbuf[0, 0, 0:3, :] = jnp.concatenate([targets_in[:, 0], targets_in[:, 1]], axis=1)
        spread = lax.broadcasted_iota(jnp.int32, (ATOMS, 128), 1) % ATOMS
        spread = jnp.where(spread == lax.broadcasted_iota(jnp.int32, (ATOMS, 128), 0), 1.0, 0.0)
        for s in range(2):
            here = slice(s * HALF, (s + 1) * HALF)
            beads = bead_in[s].astype(jnp.float32).astype(jnp.bfloat16)
            repeated[here, :] = lax.dot_general(
                beads, spread.astype(jnp.bfloat16), (((0,), (0,)), ((), ())), preferred_element_type=jnp.float32
            )
            alive = lax.broadcasted_iota(jnp.int32, (BEADS, HALF), 0) < count_in[s:s + 1, :]
            kinds = jnp.where(alive, type_in[s], -1).astype(jnp.float32).astype(jnp.bfloat16)
            same = lax.broadcasted_iota(jnp.int32, (BEADS, BEADS), 0)
            same = same == lax.broadcasted_iota(jnp.int32, (BEADS, BEADS), 1)
            kinds = lax.dot_general(
                kinds, jnp.where(same, 1.0, 0.0).astype(jnp.bfloat16), (((0,), (0,)), ((), ())),
                preferred_element_type=jnp.float32,
            )
            for i in range(HALF // GROUP):
                rows = kinds[i * GROUP:(i + 1) * GROUP]
                for b in range(BEADS):
                    live[s * (HALF // GROUP) + i, b * GROUP:(b + 1) * GROUP, :] = jnp.broadcast_to(
                        rows[:, b:b + 1], (GROUP, 128)
                    )

    bead_id = (lax.broadcasted_iota(jnp.int32, (slots, GROUP * ATOMS), 0) // GROUP).astype(jnp.float32)
    member = lax.broadcasted_iota(jnp.int32, (GROUP, GROUP * ATOMS), 1) // ATOMS
    member = member == lax.broadcasted_iota(jnp.int32, (GROUP, GROUP * ATOMS), 0)

    def unit_points():
        def body(i, carry):
            rows = pl.ds(pl.multiple_of(i * 128, 128), 128)
            wide = points[rows, :].astype(jnp.float32)
            mean = jnp.sum(wide * wide, axis=1, keepdims=True) * (1.0 / width)
            points[rows, :] = (wide * lax.rsqrt(mean + EPSILON)).astype(jnp.bfloat16)
            return carry
        lax.fori_loop(0, shard // 128, body, 0)

    def unit_beads(t):
        for i in range(per_sub):
            j = t * per_sub + i
            near_atoms = repeated[j * GROUP:(j + 1) * GROUP, :]
            own = jnp.where(member, jnp.concatenate([near_atoms, near_atoms], axis=1), -1.0)
            onehot = jnp.where(jnp.concatenate([own] * BEADS, axis=0) == bead_id, 1.0, 0.0)
            size = jnp.maximum(jnp.sum(onehot, axis=1, keepdims=True), 1.0)
            summed = jnp.dot(onehot.astype(jnp.bfloat16), atoms[j], preferred_element_type=jnp.float32)
            inverse = 1.0 / size
            mean = jnp.sum(summed * summed, axis=1, keepdims=True) * (inverse * inverse * (1.0 / width))
            scale = inverse * lax.rsqrt(mean + EPSILON)
            units[compute_order.index(t) % 2, i * slots:(i + 1) * slots, :] = (summed * scale).astype(jnp.bfloat16)

    def kernel_rows(t):
        route, sub = t // 2, t % 2
        tile = 256
        for cols in (slice(i, i + tile) for i in range(0, shard, tile)):
            scores = lax.dot_general(
                units[compute_order.index(t) % 2], points[cols, :], (((1,), (1,)), ((), ())), preferred_element_type=jnp.float32,
            )
            kind = ptype[:, cols].astype(jnp.float32)
            parts = []
            for i in range(per_sub):
                j = t * per_sub + i
                part = jnp.exp2(scores[i * slots:(i + 1) * slots] * (LOG2E * width ** (-0.5)))
                alive = live[j]
                part = jnp.where(jnp.concatenate([alive] * (tile // 128), axis=1) == kind, part, 0.0)
                parts.append(jnp.sum(part.reshape(BEADS, GROUP, tile), axis=0))
            kbuf[route, 0, sub * SUB:(sub + 1) * SUB, cols] = jnp.concatenate(parts, axis=0).astype(jnp.bfloat16)

    groups = [(route, outer) for outer in (0, 3, 1, 2) for route in (0, 1)]
    index_of = {group: g for g, group in enumerate(groups)}

    def relative(route, step_x, step_z):
        return (step_z % SIDE, step_x % SIDE) if route == 0 else (step_x % SIDE, step_z % SIDE)

    def direct(route, n, to_x, to_z, s):
        outer, inner = relative(route, -to_x, -to_z)
        lanes = pl.ds(pl.multiple_of(s * STRIP, STRIP), STRIP)
        return remote(
            kbuf.at[route, 0, pl.ds(0, HALF), lanes],
            rbuf.at[route, outer, pl.ds(inner * HALF, HALF), :],
            d_send.at[route * 15 + n],
            d_recv.at[(route * SIDE + outer) * SIDE + inner],
            on_plane(to_x, to_z),
        )

    def direct_each(route, do):
        for n, (to_x, to_z) in enumerate(offsets):
            there_x, there_z = (x + to_x) % SIDE, (z + to_z) % SIDE

            @pl.when(there_x // 2 == col)
            def _():
                do(direct(route, n, to_x, to_z, (there_x % 2) * SIDE + there_z))

    def strip(g, r):
        return sbuf.at[g, pl.ds(pl.multiple_of(r * STRIP, STRIP), STRIP), :]

    def strip_copy(g, r, which, peer):
        here = strip(g, r)
        return remote(here, here, s_send.at[g * 4 + which], s_recv.at[g * 4 + r], peer)

    def strip_arrived(g, r):
        strip_copy(g, r, 0, sibling).wait_recv()

    def strip_send(group):
        g = index_of[group]
        route, outer = group

        @pl.when(owner)
        def _():
            for inner in range(SIDE):
                if (outer, inner) == (0, 0):
                    lanes = pl.ds(pl.multiple_of(at_strip * STRIP, STRIP), STRIP)
                    rbuf[route, 0, 0:HALF, :] = kbuf[route, 0, 0:HALF, lanes]
                else:
                    here = rbuf.at[route, outer, pl.ds(inner * HALF, HALF), :]
                    remote(
                        here, here, d_send.at[0], d_recv.at[(route * SIDE + outer) * SIDE + inner], sibling
                    ).wait_recv()
            sbuf[g, pl.ds(pl.multiple_of(row * STRIP, STRIP), STRIP), :] = rbuf[route, outer].T
            strip_copy(g, row, 0, up).start()
            strip_copy(g, row, 1, down).start()
            strip_copy(g, row, 2, sibling).start()

    def strip_relay(group):
        g = index_of[group]
        r_up, r_down = h_up * 2 + core, h_down * 2 + core

        @pl.when(jnp.logical_not(owner))
        def _():
            strip_arrived(g, r_down)
            strip_arrived(g, r_up)

            @pl.when(h == (g // 2) % 2)
            def _():
                strip_copy(g, r_down, 2, up).start()
                strip_copy(g, r_up, 3, down).start()
            strip_copy(g, r_down, 0, sibling).start()
            strip_copy(g, r_up, 1, sibling).start()

    def strip_last(group):
        g = index_of[group]
        other = (1 - h) * 2 + core

        @pl.when(owner)
        def _():
            strip_arrived(g, other)
            strip_copy(g, other, 3, sibling).start()

    def strip_drain(group):
        g = index_of[group]
        for which in range(2):
            strip_copy(g, row, which, sibling).wait_send()

        @pl.when(jnp.logical_or(owner, h == (g // 2) % 2))
        def _():
            for which in range(2, 4):
                strip_copy(g, row, which, sibling).wait_send()

    def strips_here(group):
        g = index_of[group]
        strip_arrived(g, 1 - core)
        strip_arrived(g, 2 + 1 - core)

    def gram(group, first=False):
        g = index_of[group]
        strips_here(group)
        route, outer = group
        tile = 256

        def body(ct, carry):
            cols = pl.ds(pl.multiple_of(ct * tile, tile), tile)
            part = jnp.dot(sbuf[g], kbuf[route, outer, :, cols], preferred_element_type=jnp.float32)
            if first:
                acc[:, cols] = part
            else:
                acc[:, cols] += part
            return carry
        lax.fori_loop(0, shard // tile, body, 0)

    def weight_copy(axis, step):
        if axis == 0:
            src, dst, peer = wbuf.at[0, 0], wbuf.at[0, (-step) % SIDE], on_x(step)
        else:
            src, dst, peer = wbuf.at[0], wbuf.at[(-step) % SIDE], on_z(step)
        i = axis * 3 + step - 1
        return remote(src, dst, w_send.at[i], w_recv.at[i], peer)

    def weight_rows():
        low = lax.broadcasted_iota(jnp.int32, (8, 128), 1) < HALF
        for (route, outer), g in index_of.items():
            if route == 0:
                parts = [wbuf[outer, i] for i in range(SIDE)]
                pairs = [jnp.where(low, parts[i], pltpu.roll(parts[i + 1], HALF, 1)) for i in (0, 2)]
            else:
                parts = [wbuf[i, outer] for i in range(SIDE)]
                pairs = [jnp.where(low, pltpu.roll(parts[i], HALF, 1), parts[i + 1]) for i in (0, 2)]
            wide = jnp.concatenate(pairs, axis=1)
            high = wide.astype(jnp.bfloat16).astype(jnp.float32)
            both = jnp.concatenate([high, wide - high], axis=0)
            sbuf[g, 4 * STRIP:, :] = both.astype(jnp.bfloat16)

    prepare()
    load_points.wait()
    unit_points()
    loads[0].wait()
    unit_beads(0)

    def compute(n):
        if n + 1 < 4:
            loads[n + 1].wait()
            unit_beads(compute_order[n + 1])
        kernel_rows(compute_order[n])

    def gather_rest(route, outer):
        for inner in (0, 3, 1, 2):
            for sub in {0: (), 3: (1,), 1: (0,), 2: (0, 1)}[outer]:
                arrived(route, outer, inner, sub)

    compute(0)
    pl.semaphore_wait(barrier, len(peers))
    send_own(0, 0)
    compute(1)
    direct_each(0, lambda copy: copy.start())
    for step in (1, 2, 3):
        weight_copy(0, step).start()
    send_own(0, 1)
    compute(2)
    send_own(1, 0)
    compute(3)
    direct_each(1, lambda copy: copy.start())
    send_own(1, 1)
    strip_send((0, 0))
    near(1, 0)
    near(0, 0)
    strip_send((0, 1))
    strip_send((1, 0))
    strip_relay((0, 0))
    near(0, 1)
    strip_send((1, 1))
    strip_relay((0, 1))
    strip_send((0, 2))
    strip_send((1, 3))
    near(1, 1)
    for step in (1, 2, 3):
        weight_copy(0, step).wait_recv()
    for step in (1, 2, 3):
        weight_copy(1, step).start()
    strip_relay((1, 0))
    strip_send((0, 3))
    strip_last((0, 0))
    middle(1, 0)
    middle(0, 0)
    middle(0, 1)
    strip_last((1, 0))
    strip_relay((1, 1))
    strip_last((0, 1))
    strip_relay((0, 2))
    strip_send((1, 2))
    middle(1, 1)
    strip_relay((0, 3))
    far(0, 0)
    strip_relay((1, 3))
    for step in (1, 2, 3):
        weight_copy(1, step).wait_recv()
    weight_rows()
    gather_rest(1, 0)
    gram((1, 0), first=True)
    gather_rest(0, 0)
    gram((0, 0))
    strip_relay((1, 2))
    strip_last((1, 1))
    far(0, 1)
    gather_rest(0, 1)
    gram((0, 1))
    strip_last((0, 3))
    far(1, 0)
    far(1, 1)
    strip_last((1, 3))
    strip_last((0, 2))
    gather_rest(1, 1)
    gram((1, 1))
    gather_rest(0, 3)
    gram((0, 3))
    strip_last((1, 2))
    gather_rest(1, 3)
    gram((1, 3))
    for route in (0, 1):
        gather_rest(route, 2)
        strips_here((route, 2))

    def finish(rows, cols):
        value = acc[rows, cols]
        for route in (0, 1):
            g = index_of[(route, 2)]
            value += jnp.dot(sbuf[g, rows, :], kbuf[route, 2, :, cols], preferred_element_type=jnp.float32)
        return value * (1.0 / total)

    def block(r):
        rows = pl.ds(pl.multiple_of(r * STRIP, STRIP), STRIP)
        obuf[r] = finish(rows, pl.ds(0, shard)).astype(jnp.bfloat16)

    across = (1 - h) * 2

    def out_copy(r, which, peer):
        return remote(obuf.at[r], gram_out.at[row], o_send.at[which], o_recv.at[row], peer)

    def out_done(r, which):
        copy = remote(obuf.at[r], gram_out.at[r], o_send.at[which], o_recv.at[r], sibling)
        copy.wait_send()
        copy.wait_recv()

    def turned(s, k, do_remote, do_local):
        there = gram_out.at[across + k, :, pl.ds(pl.multiple_of(at_strip * STRIP, STRIP), STRIP)]

        @pl.when(dp != 8 * col + s)
        def _():
            peer = {"dp": 8 * col + s, "row": row, "col": col}
            do_remote(remote(tbuf.at[s, k], there, t_send.at[2 * s + k], t_recv.at[2 * at_strip + k], peer))

        @pl.when(dp == 8 * col + s)
        def _():
            do_local(pltpu.make_async_copy(tbuf.at[s, k], there, t_send.at[2 * s + k]))

    def turned_arrived(s, k):
        @pl.when(dp != 8 * col + s)
        def _():
            there = gram_out.at[across + k, :, pl.ds(s * STRIP, STRIP)]
            remote(tbuf.at[s, k], there, t_send.at[2 * s + k], t_recv.at[2 * s + k], sibling).wait_recv()

    def start(copy):
        copy.start()

    def turn(at_col):
        return TURNS[0] + (TURNS[1] - TURNS[0]) * at_col

    def straight(k):
        rows = pl.ds(DIRECT, STRIP - DIRECT)
        return remote(
            obuf.at[across + k, rows], gram_out.at[row, rows], o_send.at[k], o_recv.at[row], on_y(2, k)
        )

    def straight_done(k):
        rows = pl.ds(DIRECT, STRIP - DIRECT)
        copy = remote(
            obuf.at[across + k, rows], gram_out.at[across + k, rows], o_send.at[k], o_recv.at[across + k], sibling
        )
        copy.wait_send()
        copy.wait_recv()

    def first_leg(k, i):
        rows = pl.ds(*RELAYED[i])
        return remote(
            obuf.at[across + k, rows], relay.at[k, rows], y_send.at[2 * k + i], y_recv.at[2 * k + i],
            on_y(turn(col), core),
        )

    def second_leg(k, i):
        rows = pl.ds(*RELAYED[i])
        way = turn(1 - col)
        source = ((y - way + SIDE) % SIDE) // 2 * 2 + core
        return remote(
            relay.at[k, rows], gram_out.at[source, rows], f_send.at[2 * k + i], f_recv.at[2 * core + i],
            on_y(way, k),
        )

    def relayed_arrived(k, i):
        here = gram_out.at[across + k, pl.ds(*RELAYED[i])]
        remote(here, here, y_send.at[0], f_recv.at[2 * k + i], sibling).wait_recv()

    for k in range(2):
        block(across + k)

        @pl.when(jnp.logical_not(owner))
        def _():
            for i in range(2):
                first_leg(k, i).start()
            straight(k).start()

        @pl.when(owner)
        def _():
            for s in range(8):
                tbuf[s, k] = obuf[across + k, :, s * STRIP:(s + 1) * STRIP].T
                turned(s, k, start, start)
    block(h * 2 + 1 - core)
    out_copy(h * 2 + 1 - core, 2, sibling).start()

    @pl.when(owner)
    def _():
        for k in range(2):
            for i in range(2):
                first_leg(k, i).wait_recv()
                second_leg(k, i).start()
    block(row)
    keep = pltpu.make_async_copy(obuf.at[row], gram_out.at[row], o_local)
    keep.start()
    tail = finish(pl.ds(4 * STRIP, 16), pl.ds(0, shard))
    rhs_out[...] = tail[0:8] + tail[8:16]
    for copy in pending:
        copy.wait_send()
    for route in (0, 1):
        direct_each(route, lambda copy: copy.wait_send())
    for group in groups:
        strip_drain(group)
    for axis in (0, 1):
        for step in (1, 2, 3):
            weight_copy(axis, step).wait_send()
    keep.wait()
    out_done(h * 2 + 1 - core, 2)

    @pl.when(jnp.logical_not(owner))
    def _():
        for k in range(2):
            straight_done(k)
            for i in range(2):
                first_leg(k, i).wait_send()
                relayed_arrived(k, i)

    @pl.when(owner)
    def _():
        for k in range(2):
            for i in range(2):
                second_leg(k, i).wait_send()
        for s in range(8):
            for k in range(2):
                turned(s, k, lambda copy: copy.wait_send(), lambda copy: copy.wait())
                turned_arrived(s, k)


def widen(gram_in, rhs_in, gram_out, rhs_out):
    for q in range(4):
        gram_out[:, q, :] = gram_in[q].astype(jnp.float32)
    rhs_out[...] = rhs_in[0:3, :]


def shards(atom_feats, atom_bead, bead_count, bead_type, sparse_points, sparse_type, targets):
    slabs, local, atoms, width = atom_feats.shape
    config_rows = slabs * local
    shard = sparse_points.shape[0]
    total = config_rows * lax.axis_size("dp")
    blocks = config_rows // GROUP
    bf16, f32, i32 = jnp.bfloat16, jnp.float32, jnp.int32
    dma = pltpu.SemaphoreType.DMA
    vmem = pl.BlockSpec(memory_space=pltpu.VMEM)
    hbm = pl.BlockSpec(memory_space=pltpu.HBM)
    gram, rhs = pl.pallas_call(
        functools.partial(kernel, total),
        out_shape=(
            jax.ShapeDtypeStruct((4, STRIP, shard), bf16),
            jax.ShapeDtypeStruct((8, shard), f32),
        ),
        in_specs=[hbm] * 7,
        out_specs=(hbm, vmem),
        scratch_shapes=[
            pltpu.VMEM((blocks, GROUP * atoms, width), bf16),
            pltpu.VMEM((shard, width), bf16),
            pltpu.VMEM((2, SUB * BEADS, width), bf16),
            pltpu.VMEM((2, SIDE, SIDE * HALF, shard), bf16),
            pltpu.VMEM((2, SIDE, SIDE * HALF, STRIP), bf16),
            pltpu.VMEM((8, 4 * STRIP + 16, SIDE * HALF), bf16),
            pltpu.VMEM((SIDE, SIDE, 8, 128), f32),
            pltpu.VMEM((4 * STRIP + 16, shard), f32),
            pltpu.VMEM((4, STRIP, shard), bf16),
            pltpu.VMEM((8, 2, STRIP, STRIP), bf16),
            pltpu.VMEM((2, DIRECT, shard), bf16),
            pltpu.VMEM((slabs, atoms, local), i32),
            pltpu.VMEM(bead_count.shape, i32),
            pltpu.VMEM((slabs, BEADS, local), i32),
            pltpu.VMEM((1, shard), i32),
            pltpu.VMEM((3, slabs, local), f32),
            pltpu.VMEM((config_rows, 128), f32),
            pltpu.VMEM((blocks, BEADS * GROUP, 128), f32),
            dma((10,)),
            dma((60,)),
            dma((64,)),
            dma((30,)),
            dma((32,)),
            dma((32,)),
            dma((32,)),
            dma((6,)),
            dma((6,)),
            dma((3,)),
            dma((4,)),
            dma,
            dma((16,)),
            dma((16,)),
            dma((4,)),
            dma((4,)),
            dma((4,)),
            dma((4,)),
        ],
        compiler_params=pltpu.CompilerParams(
            collective_id=0, has_side_effects=True, vmem_limit_bytes=60 * 1024 * 1024
        ),
    )(
        atom_feats.reshape(blocks, GROUP * atoms, width), sparse_points, jnp.swapaxes(atom_bead, 1, 2),
        bead_count, jnp.swapaxes(bead_type, 1, 2), sparse_type.reshape(1, shard), jnp.swapaxes(targets, 0, 1),
    )
    steps = 2
    return pl.pallas_call(
        widen,
        grid=(steps,),
        out_shape=(
            jax.ShapeDtypeStruct((STRIP, 4, shard), f32),
            jax.ShapeDtypeStruct((3, shard), f32),
        ),
        in_specs=[
            pl.BlockSpec((4, STRIP // steps, shard), lambda i: (0, i, 0)),
            pl.BlockSpec((8, shard), lambda i: (0, 0)),
        ],
        out_specs=(
            pl.BlockSpec((STRIP // steps, 4, shard), lambda i: (i, 0, 0)),
            pl.BlockSpec((3, shard), lambda i: (0, 0)),
        ),
        compiler_params=pltpu.CompilerParams(vmem_limit_bytes=60 * 1024 * 1024),
    )(gram, rhs)


def solution(mesh):
    return jax.shard_map(
        shards,
        mesh=mesh,
        in_specs=(
            P(None, "dp", None, None),
            P(None, "dp", None),
            P(None, "dp"),
            P(None, "dp", None),
            P(("row", "col"), None),
            P(("row", "col")),
            P(None, None, "dp"),
        ),
        out_specs=(P(("row", "dp"), None, "col"), P(None, ("row", "col"))),
        check_vma=False,
    )
```

```python
import functools

import jax
import jax.numpy as jnp
from jax import lax
from jax.experimental import pallas as pl
from jax.experimental.pallas import tpu as pltpu
from jax.sharding import PartitionSpec as P

EPSILON = 1e-06
MESH = pl.DeviceIdType.MESH
LOG2E = 1.4426950408889634

SIDE = 4
GROUP = 8
SUB = 32
HALF = 2 * SUB
STRIP = 128
ATOMS = 32
BEADS = 16
RELAYED = ((0, 32), (32, 16))
DIRECT = 48
TURNS = (-1, 1)


def kernel(
    total,
    atoms_hbm, points_hbm, bead_hbm, count_hbm, type_hbm, ptype_hbm, targets_hbm,
    gram_out, rhs_out,
    atoms, points, units, kbuf, rbuf, sbuf, wbuf, acc, obuf, tbuf, relay,
    bead_in, count_in, type_in, ptype, targets_in, repeated, live,
    load_sem, k_send, k_recv, d_send, d_recv, s_send, s_recv, w_send, w_recv, o_send, o_recv, o_local, t_send, t_recv, y_send, y_recv, f_send, f_recv,
):
    width = points.shape[1]
    shard = points.shape[0]
    slots = BEADS * GROUP
    dp = lax.axis_index("dp")
    row = lax.axis_index("row")
    col = lax.axis_index("col")
    x, z = dp // SIDE, dp % SIDE
    h, core = row // 2, row % 2
    y = h * 2 + col
    at_strip = dp % 8
    owner = (dp // 8) == col

    def on_plane(step_x, step_z):
        return {"dp": ((x + step_x) % SIDE) * SIDE + (z + step_z) % SIDE, "row": row, "col": col}

    def on_x(step):
        return on_plane(step, 0)

    def on_z(step):
        return on_plane(0, step)

    def on_y(step, at_core):
        to = (y + step) % SIDE
        return {"dp": dp, "row": (to // 2) * 2 + at_core, "col": to % 2}

    sibling = on_y(0, 1 - core)
    up, down = on_y(1, core), on_y(-1, core)
    h_up, h_down = ((y + 1) % SIDE) // 2, ((y - 1) % SIDE) // 2
    offsets = [(i, j) for i in range(SIDE) for j in range(SIDE) if (i, j) != (0, 0)]

    loads = []
    compute_order = order = (0, 1, 2, 3)
    per_sub = SUB // GROUP
    small = []
    for i, (src, dst) in enumerate((
        (bead_hbm, bead_in), (count_hbm, count_in), (type_hbm, type_in), (ptype_hbm, ptype),
        (targets_hbm, targets_in),
    )):
        copy = pltpu.make_async_copy(src, dst, load_sem.at[5 + i])
        copy.start()
        small.append(copy)
    load_points = pltpu.make_async_copy(points_hbm, points, load_sem.at[4])
    load_points.start()
    for t in order:
        rows = pl.ds(t * per_sub, per_sub)
        copy = pltpu.make_async_copy(atoms_hbm.at[rows], atoms.at[rows], load_sem.at[t])
        copy.start()
        loads.append(copy)

    barrier = pltpu.get_barrier_semaphore()
    peers = [on_plane(*offset) for offset in offsets]
    peers += [sibling, up, down, on_y(2, core), on_y(2, 1 - core)]
    for peer in peers:
        pl.semaphore_signal(barrier, inc=1, device_id=peer, device_id_type=MESH)

    pending = []

    def remote(src, dst, send, recv, peer):
        return pltpu.make_async_remote_copy(
            src_ref=src, dst_ref=dst, send_sem=send, recv_sem=recv,
            device_id=peer, device_id_type=MESH,
        )

    def slot(route, outer, inner, sub):
        return kbuf.at[route, outer % SIDE, pl.ds((inner % SIDE) * HALF + sub * SUB, SUB), :]

    def recv_sem(route, outer, inner, sub):
        return k_recv.at[((route * SIDE + outer % SIDE) * SIDE + inner % SIDE) * 2 + sub]

    def along(route, phase, step):
        return on_x(step) if (route == 0) == (phase == 0) else on_z(step)

    def send(route, outer, inner, sub, phase, step):
        if phase == 0:
            to = (route, outer, inner - step, sub)
        else:
            to = (route, outer - step, inner, sub)
        copy = remote(
            slot(route, outer, inner, sub), slot(*to), k_send.at[len(pending)], recv_sem(*to),
            along(route, phase, step),
        )
        copy.start()
        pending.append(copy)

    def arrived(route, outer, inner, sub):
        here = slot(route, outer, inner, sub)
        remote(here, here, k_send.at[0], recv_sem(route, outer, inner, sub), sibling).wait_recv()

    def send_own(route, sub):
        for step in (1, -1):
            send(route, 0, 0, sub, 0, step)
        for step in (1, -1):
            send(route, 0, 0, sub, 1, step)

    def inner_step(route, inner, sub):
        arrived(route, 0, inner, sub)
        if inner == 3 and sub == 0:
            send(route, 0, inner, sub, 0, 1)
        if inner == 1 and sub == 1:
            send(route, 0, inner, sub, 0, -1)
        for step in (1, -1):
            send(route, 0, inner, sub, 1, step)

    def outer_step(route, inner, sub):
        if sub == 0:
            arrived(route, 3, inner, 0)
            send(route, 3, inner, 0, 1, 1)
        else:
            arrived(route, 1, inner, 1)
            send(route, 1, inner, 1, 1, -1)

    def near(route, sub):
        for inner in (3, 1) if sub == 0 else (1, 3):
            inner_step(route, inner, sub)
        outer_step(route, 0, sub)

    def middle(route, sub):
        inner_step(route, 2, sub)
        outer_step(route, 3, sub)
        outer_step(route, 1, sub)

    def far(route, sub):
        outer_step(route, 2, sub)

    def prepare():
        for copy in small:
            copy.wait()
        wbuf[0, 0] = jnp.zeros_like(wbuf[0, 0])
        wbuf[0, 0, 0:3, :] = jnp.concatenate([targets_in[:, 0], targets_in[:, 1]], axis=1)
        spread = lax.broadcasted_iota(jnp.int32, (ATOMS, 128), 1) % ATOMS
        spread = jnp.where(spread == lax.broadcasted_iota(jnp.int32, (ATOMS, 128), 0), 1.0, 0.0)
        for s in range(2):
            here = slice(s * HALF, (s + 1) * HALF)
            beads = bead_in[s].astype(jnp.float32).astype(jnp.bfloat16)
            repeated[here, :] = lax.dot_general(
                beads, spread.astype(jnp.bfloat16), (((0,), (0,)), ((), ())), preferred_element_type=jnp.float32
            )
            alive = lax.broadcasted_iota(jnp.int32, (BEADS, HALF), 0) < count_in[s:s + 1, :]
            kinds = jnp.where(alive, type_in[s], -1).astype(jnp.float32).astype(jnp.bfloat16)
            same = lax.broadcasted_iota(jnp.int32, (BEADS, BEADS), 0)
            same = same == lax.broadcasted_iota(jnp.int32, (BEADS, BEADS), 1)
            kinds = lax.dot_general(
                kinds, jnp.where(same, 1.0, 0.0).astype(jnp.bfloat16), (((0,), (0,)), ((), ())),
                preferred_element_type=jnp.float32,
            )
            for i in range(HALF // GROUP):
                rows = kinds[i * GROUP:(i + 1) * GROUP]
                for b in range(BEADS):
                    live[s * (HALF // GROUP) + i, b * GROUP:(b + 1) * GROUP, :] = jnp.broadcast_to(
                        rows[:, b:b + 1], (GROUP, 128)
                    )

    bead_id = (lax.broadcasted_iota(jnp.int32, (slots, GROUP * ATOMS), 0) // GROUP).astype(jnp.float32)
    member = lax.broadcasted_iota(jnp.int32, (GROUP, GROUP * ATOMS), 1) // ATOMS
    member = member == lax.broadcasted_iota(jnp.int32, (GROUP, GROUP * ATOMS), 0)

    def unit_points():
        def body(i, carry):
            rows = pl.ds(pl.multiple_of(i * 128, 128), 128)
            wide = points[rows, :].astype(jnp.float32)
            mean = jnp.sum(wide * wide, axis=1, keepdims=True) * (1.0 / width)
            points[rows, :] = (wide * lax.rsqrt(mean + EPSILON)).astype(jnp.bfloat16)
            return carry
        lax.fori_loop(0, shard // 128, body, 0)

    def unit_beads(t):
        for i in range(per_sub):
            j = t * per_sub + i
            near_atoms = repeated[j * GROUP:(j + 1) * GROUP, :]
            own = jnp.where(member, jnp.concatenate([near_atoms, near_atoms], axis=1), -1.0)
            onehot = jnp.where(jnp.concatenate([own] * BEADS, axis=0) == bead_id, 1.0, 0.0)
            size = jnp.maximum(jnp.sum(onehot, axis=1, keepdims=True), 1.0)
            summed = jnp.dot(onehot.astype(jnp.bfloat16), atoms[j], preferred_element_type=jnp.float32)
            inverse = 1.0 / size
            mean = jnp.sum(summed * summed, axis=1, keepdims=True) * (inverse * inverse * (1.0 / width))
            scale = inverse * lax.rsqrt(mean + EPSILON)
            units[compute_order.index(t) % 2, i * slots:(i + 1) * slots, :] = (summed * scale).astype(jnp.bfloat16)

    def kernel_rows(t):
        route, sub = t // 2, t % 2
        tile = 256
        for cols in (slice(i, i + tile) for i in range(0, shard, tile)):
            scores = lax.dot_general(
                units[compute_order.index(t) % 2], points[cols, :], (((1,), (1,)), ((), ())), preferred_element_type=jnp.float32,
            )
            kind = ptype[:, cols].astype(jnp.float32)
            parts = []
            for i in range(per_sub):
                j = t * per_sub + i
                part = jnp.exp2(scores[i * slots:(i + 1) * slots] * (LOG2E * width ** (-0.5)))
                alive = live[j]
                part = jnp.where(jnp.concatenate([alive] * (tile // 128), axis=1) == kind, part, 0.0)
                parts.append(jnp.sum(part.reshape(BEADS, GROUP, tile), axis=0))
            kbuf[route, 0, sub * SUB:(sub + 1) * SUB, cols] = jnp.concatenate(parts, axis=0).astype(jnp.bfloat16)

    groups = [(route, outer) for outer in (0, 3, 1, 2) for route in (0, 1)]
    index_of = {group: g for g, group in enumerate(groups)}

    def relative(route, step_x, step_z):
        return (step_z % SIDE, step_x % SIDE) if route == 0 else (step_x % SIDE, step_z % SIDE)

    def direct(route, n, to_x, to_z, s):
        outer, inner = relative(route, -to_x, -to_z)
        lanes = pl.ds(pl.multiple_of(s * STRIP, STRIP), STRIP)
        return remote(
            kbuf.at[route, 0, pl.ds(0, HALF), lanes],
            rbuf.at[route, outer, pl.ds(inner * HALF, HALF), :],
            d_send.at[route * 15 + n],
            d_recv.at[(route * SIDE + outer) * SIDE + inner],
            on_plane(to_x, to_z),
        )

    def direct_each(route, do):
        for n, (to_x, to_z) in enumerate(offsets):
            there_x, there_z = (x + to_x) % SIDE, (z + to_z) % SIDE

            @pl.when(there_x // 2 == col)
            def _():
                do(direct(route, n, to_x, to_z, (there_x % 2) * SIDE + there_z))

    def strip(g, r):
        return sbuf.at[g, pl.ds(pl.multiple_of(r * STRIP, STRIP), STRIP), :]

    def strip_copy(g, r, which, peer):
        here = strip(g, r)
        return remote(here, here, s_send.at[g * 4 + which], s_recv.at[g * 4 + r], peer)

    def strip_arrived(g, r):
        strip_copy(g, r, 0, sibling).wait_recv()

    def strip_send(group):
        g = index_of[group]
        route, outer = group

        @pl.when(owner)
        def _():
            for inner in range(SIDE):
                if (outer, inner) == (0, 0):
                    lanes = pl.ds(pl.multiple_of(at_strip * STRIP, STRIP), STRIP)
                    rbuf[route, 0, 0:HALF, :] = kbuf[route, 0, 0:HALF, lanes]
                else:
                    here = rbuf.at[route, outer, pl.ds(inner * HALF, HALF), :]
                    remote(
                        here, here, d_send.at[0], d_recv.at[(route * SIDE + outer) * SIDE + inner], sibling
                    ).wait_recv()
            sbuf[g, pl.ds(pl.multiple_of(row * STRIP, STRIP), STRIP), :] = rbuf[route, outer].T
            strip_copy(g, row, 0, up).start()
            strip_copy(g, row, 1, down).start()
            strip_copy(g, row, 2, sibling).start()

    def strip_relay(group):
        g = index_of[group]
        r_up, r_down = h_up * 2 + core, h_down * 2 + core

        @pl.when(jnp.logical_not(owner))
        def _():
            strip_arrived(g, r_down)
            strip_arrived(g, r_up)

            @pl.when(h == (g // 2) % 2)
            def _():
                strip_copy(g, r_down, 2, up).start()
                strip_copy(g, r_up, 3, down).start()
            strip_copy(g, r_down, 0, sibling).start()
            strip_copy(g, r_up, 1, sibling).start()

    def strip_last(group):
        g = index_of[group]
        other = (1 - h) * 2 + core

        @pl.when(owner)
        def _():
            strip_arrived(g, other)
            strip_copy(g, other, 3, sibling).start()

    def strip_drain(group):
        g = index_of[group]
        for which in range(2):
            strip_copy(g, row, which, sibling).wait_send()

        @pl.when(jnp.logical_or(owner, h == (g // 2) % 2))
        def _():
            for which in range(2, 4):
                strip_copy(g, row, which, sibling).wait_send()

    def strips_here(group):
        g = index_of[group]
        strip_arrived(g, 1 - core)
        strip_arrived(g, 2 + 1 - core)

    def gram(group, first=False):
        g = index_of[group]
        strips_here(group)
        route, outer = group
        tile = 256

        def body(ct, carry):
            cols = pl.ds(pl.multiple_of(ct * tile, tile), tile)
            part = jnp.dot(sbuf[g], kbuf[route, outer, :, cols], preferred_element_type=jnp.float32)
            if first:
                acc[:, cols] = part
            else:
                acc[:, cols] += part
            return carry
        lax.fori_loop(0, shard // tile, body, 0)

    def weight_copy(axis, step):
        if axis == 0:
            src, dst, peer = wbuf.at[0, 0], wbuf.at[0, (-step) % SIDE], on_x(step)
        else:
            src, dst, peer = wbuf.at[0], wbuf.at[(-step) % SIDE], on_z(step)
        i = axis * 3 + step - 1
        return remote(src, dst, w_send.at[i], w_recv.at[i], peer)

    def weight_rows():
        low = lax.broadcasted_iota(jnp.int32, (8, 128), 1) < HALF
        for (route, outer), g in index_of.items():
            if route == 0:
                parts = [wbuf[outer, i] for i in range(SIDE)]
                pairs = [jnp.where(low, parts[i], pltpu.roll(parts[i + 1], HALF, 1)) for i in (0, 2)]
            else:
                parts = [wbuf[i, outer] for i in range(SIDE)]
                pairs = [jnp.where(low, pltpu.roll(parts[i], HALF, 1), parts[i + 1]) for i in (0, 2)]
            wide = jnp.concatenate(pairs, axis=1)
            high = wide.astype(jnp.bfloat16).astype(jnp.float32)
            both = jnp.concatenate([high, wide - high], axis=0)
            sbuf[g, 4 * STRIP:, :] = both.astype(jnp.bfloat16)

    prepare()
    load_points.wait()
    unit_points()
    loads[0].wait()
    unit_beads(0)

    def compute(n):
        if n + 1 < 4:
            loads[n + 1].wait()
            unit_beads(compute_order[n + 1])
        kernel_rows(compute_order[n])

    def gather_rest(route, outer):
        for inner in (0, 3, 1, 2):
            for sub in {0: (), 3: (1,), 1: (0,), 2: (0, 1)}[outer]:
                arrived(route, outer, inner, sub)

    compute(0)
    pl.semaphore_wait(barrier, len(peers))
    send_own(0, 0)
    compute(1)
    direct_each(0, lambda copy: copy.start())
    for step in (1, 2, 3):
        weight_copy(0, step).start()
    send_own(0, 1)
    compute(2)
    send_own(1, 0)
    compute(3)
    send_own(1, 1)
    direct_each(1, lambda copy: copy.start())
    strip_send((0, 1))
    strip_send((0, 2))
    strip_send((0, 0))
    strip_send((0, 3))
    near(1, 0)
    near(0, 0)
    strip_send((1, 0))
    strip_relay((0, 1))
    near(0, 1)
    strip_relay((0, 0))
    strip_relay((0, 2))
    near(1, 1)
    for step in (1, 2, 3):
        weight_copy(0, step).wait_recv()
    for step in (1, 2, 3):
        weight_copy(1, step).start()
    strip_relay((0, 3))
    strip_relay((1, 0))
    strip_send((1, 3))
    strip_send((1, 2))
    strip_send((1, 1))
    middle(1, 0)
    middle(0, 0)
    strip_relay((1, 3))
    strip_last((0, 0))
    middle(0, 1)
    strip_relay((1, 2))
    middle(1, 1)
    strip_relay((1, 1))
    strip_last((0, 1))
    strip_last((1, 0))
    for step in (1, 2, 3):
        weight_copy(1, step).wait_recv()
    weight_rows()
    gather_rest(0, 0)
    gram((0, 0), first=True)
    gather_rest(1, 0)
    gram((1, 0))
    far(1, 0)
    strip_last((0, 3))
    far(0, 1)
    strip_last((1, 3))
    strip_last((0, 2))
    far(0, 0)
    gather_rest(0, 1)
    gram((0, 1))
    far(1, 1)
    strip_last((1, 1))
    gather_rest(1, 3)
    gram((1, 3))
    strip_last((1, 2))
    gather_rest(0, 3)
    gram((0, 3))
    gather_rest(1, 1)
    gram((1, 1))
    for route in (0, 1):
        gather_rest(route, 2)
        strips_here((route, 2))

    def finish(rows, cols):
        value = acc[rows, cols]
        for route in (0, 1):
            g = index_of[(route, 2)]
            value += jnp.dot(sbuf[g, rows, :], kbuf[route, 2, :, cols], preferred_element_type=jnp.float32)
        return value * (1.0 / total)

    def block(r):
        rows = pl.ds(pl.multiple_of(r * STRIP, STRIP), STRIP)
        obuf[r] = finish(rows, pl.ds(0, shard)).astype(jnp.bfloat16)

    across = (1 - h) * 2

    def out_copy(r, which, peer):
        return remote(obuf.at[r], gram_out.at[row], o_send.at[which], o_recv.at[row], peer)

    def out_done(r, which):
        copy = remote(obuf.at[r], gram_out.at[r], o_send.at[which], o_recv.at[r], sibling)
        copy.wait_send()
        copy.wait_recv()

    def turned(s, k, do_remote, do_local):
        there = gram_out.at[across + k, :, pl.ds(pl.multiple_of(at_strip * STRIP, STRIP), STRIP)]

        @pl.when(dp != 8 * col + s)
        def _():
            peer = {"dp": 8 * col + s, "row": row, "col": col}
            do_remote(remote(tbuf.at[s, k], there, t_send.at[2 * s + k], t_recv.at[2 * at_strip + k], peer))

        @pl.when(dp == 8 * col + s)
        def _():
            do_local(pltpu.make_async_copy(tbuf.at[s, k], there, t_send.at[2 * s + k]))

    def turned_arrived(s, k):
        @pl.when(dp != 8 * col + s)
        def _():
            there = gram_out.at[across + k, :, pl.ds(s * STRIP, STRIP)]
            remote(tbuf.at[s, k], there, t_send.at[2 * s + k], t_recv.at[2 * s + k], sibling).wait_recv()

    def start(copy):
        copy.start()

    def turn(at_col):
        return TURNS[0] + (TURNS[1] - TURNS[0]) * at_col

    def straight(k):
        rows = pl.ds(DIRECT, STRIP - DIRECT)
        return remote(
            obuf.at[across + k, rows], gram_out.at[row, rows], o_send.at[k], o_recv.at[row], on_y(2, k)
        )

    def straight_done(k):
        rows = pl.ds(DIRECT, STRIP - DIRECT)
        copy = remote(
            obuf.at[across + k, rows], gram_out.at[across + k, rows], o_send.at[k], o_recv.at[across + k], sibling
        )
        copy.wait_send()
        copy.wait_recv()

    def first_leg(k, i):
        rows = pl.ds(*RELAYED[i])
        return remote(
            obuf.at[across + k, rows], relay.at[k, rows], y_send.at[2 * k + i], y_recv.at[2 * k + i],
            on_y(turn(col), core),
        )

    def second_leg(k, i):
        rows = pl.ds(*RELAYED[i])
        way = turn(1 - col)
        source = ((y - way + SIDE) % SIDE) // 2 * 2 + core
        return remote(
            relay.at[k, rows], gram_out.at[source, rows], f_send.at[2 * k + i], f_recv.at[2 * core + i],
            on_y(way, k),
        )

    def relayed_arrived(k, i):
        here = gram_out.at[across + k, pl.ds(*RELAYED[i])]
        remote(here, here, y_send.at[0], f_recv.at[2 * k + i], sibling).wait_recv()

    for k in range(2):
        block(across + k)

        @pl.when(jnp.logical_not(owner))
        def _():
            for i in range(2):
                first_leg(k, i).start()
            straight(k).start()

        @pl.when(owner)
        def _():
            for s in range(8):
                tbuf[s, k] = obuf[across + k, :, s * STRIP:(s + 1) * STRIP].T
                turned(s, k, start, start)
    block(h * 2 + 1 - core)
    out_copy(h * 2 + 1 - core, 2, sibling).start()

    @pl.when(owner)
    def _():
        for k in range(2):
            for i in range(2):
                first_leg(k, i).wait_recv()
                second_leg(k, i).start()
    block(row)
    keep = pltpu.make_async_copy(obuf.at[row], gram_out.at[row], o_local)
    keep.start()
    tail = finish(pl.ds(4 * STRIP, 16), pl.ds(0, shard))
    rhs_out[...] = tail[0:8] + tail[8:16]
    for copy in pending:
        copy.wait_send()
    for route in (0, 1):
        direct_each(route, lambda copy: copy.wait_send())
    for group in groups:
        strip_drain(group)
    for axis in (0, 1):
        for step in (1, 2, 3):
            weight_copy(axis, step).wait_send()
    keep.wait()
    out_done(h * 2 + 1 - core, 2)

    @pl.when(jnp.logical_not(owner))
    def _():
        for k in range(2):
            straight_done(k)
            for i in range(2):
                first_leg(k, i).wait_send()
                relayed_arrived(k, i)

    @pl.when(owner)
    def _():
        for k in range(2):
            for i in range(2):
                second_leg(k, i).wait_send()
        for s in range(8):
            for k in range(2):
                turned(s, k, lambda copy: copy.wait_send(), lambda copy: copy.wait())
                turned_arrived(s, k)


def widen(gram_in, rhs_in, gram_out, rhs_out):
    for q in range(4):
        gram_out[:, q, :] = gram_in[q].astype(jnp.float32)
    rhs_out[...] = rhs_in[0:3, :]


def shards(atom_feats, atom_bead, bead_count, bead_type, sparse_points, sparse_type, targets):
    slabs, local, atoms, width = atom_feats.shape
    config_rows = slabs * local
    shard = sparse_points.shape[0]
    total = config_rows * lax.axis_size("dp")
    blocks = config_rows // GROUP
    bf16, f32, i32 = jnp.bfloat16, jnp.float32, jnp.int32
    dma = pltpu.SemaphoreType.DMA
    vmem = pl.BlockSpec(memory_space=pltpu.VMEM)
    hbm = pl.BlockSpec(memory_space=pltpu.HBM)
    gram, rhs = pl.pallas_call(
        functools.partial(kernel, total),
        out_shape=(
            jax.ShapeDtypeStruct((4, STRIP, shard), bf16),
            jax.ShapeDtypeStruct((8, shard), f32),
        ),
        in_specs=[hbm] * 7,
        out_specs=(hbm, vmem),
        scratch_shapes=[
            pltpu.VMEM((blocks, GROUP * atoms, width), bf16),
            pltpu.VMEM((shard, width), bf16),
            pltpu.VMEM((2, SUB * BEADS, width), bf16),
            pltpu.VMEM((2, SIDE, SIDE * HALF, shard), bf16),
            pltpu.VMEM((2, SIDE, SIDE * HALF, STRIP), bf16),
            pltpu.VMEM((8, 4 * STRIP + 16, SIDE * HALF), bf16),
            pltpu.VMEM((SIDE, SIDE, 8, 128), f32),
            pltpu.VMEM((4 * STRIP + 16, shard), f32),
            pltpu.VMEM((4, STRIP, shard), bf16),
            pltpu.VMEM((8, 2, STRIP, STRIP), bf16),
            pltpu.VMEM((2, DIRECT, shard), bf16),
            pltpu.VMEM((slabs, atoms, local), i32),
            pltpu.VMEM(bead_count.shape, i32),
            pltpu.VMEM((slabs, BEADS, local), i32),
            pltpu.VMEM((1, shard), i32),
            pltpu.VMEM((3, slabs, local), f32),
            pltpu.VMEM((config_rows, 128), f32),
            pltpu.VMEM((blocks, BEADS * GROUP, 128), f32),
            dma((10,)),
            dma((60,)),
            dma((64,)),
            dma((30,)),
            dma((32,)),
            dma((32,)),
            dma((32,)),
            dma((6,)),
            dma((6,)),
            dma((3,)),
            dma((4,)),
            dma,
            dma((16,)),
            dma((16,)),
            dma((4,)),
            dma((4,)),
            dma((4,)),
            dma((4,)),
        ],
        compiler_params=pltpu.CompilerParams(
            collective_id=0, has_side_effects=True, vmem_limit_bytes=60 * 1024 * 1024
        ),
    )(
        atom_feats.reshape(blocks, GROUP * atoms, width), sparse_points, jnp.swapaxes(atom_bead, 1, 2),
        bead_count, jnp.swapaxes(bead_type, 1, 2), sparse_type.reshape(1, shard), jnp.swapaxes(targets, 0, 1),
    )
    steps = 2
    return pl.pallas_call(
        widen,
        grid=(steps,),
        out_shape=(
            jax.ShapeDtypeStruct((STRIP, 4, shard), f32),
            jax.ShapeDtypeStruct((3, shard), f32),
        ),
        in_specs=[
            pl.BlockSpec((4, STRIP // steps, shard), lambda i: (0, i, 0)),
            pl.BlockSpec((8, shard), lambda i: (0, 0)),
        ],
        out_specs=(
            pl.BlockSpec((STRIP // steps, 4, shard), lambda i: (i, 0, 0)),
            pl.BlockSpec((3, shard), lambda i: (0, 0)),
        ),
        compiler_params=pltpu.CompilerParams(vmem_limit_bytes=60 * 1024 * 1024),
    )(gram, rhs)


def solution(mesh):
    return jax.shard_map(
        shards,
        mesh=mesh,
        in_specs=(
            P(None, "dp", None, None),
            P(None, "dp", None),
            P(None, "dp"),
            P(None, "dp", None),
            P(("row", "col"), None),
            P(("row", "col")),
            P(None, None, "dp"),
        ),
        out_specs=(P(("row", "dp"), None, "col"), P(None, ("row", "col"))),
        check_vma=False,
    )
```

```python
import functools

import jax
import jax.numpy as jnp
from jax import lax
from jax.experimental import pallas as pl
from jax.experimental.pallas import tpu as pltpu
from jax.sharding import PartitionSpec as P

EPSILON = 1e-06
MESH = pl.DeviceIdType.MESH
LOG2E = 1.4426950408889634

SIDE = 4
GROUP = 8
SUB = 32
HALF = 2 * SUB
STRIP = 128
ATOMS = 32
BEADS = 16
RELAYED = ((0, 32), (32, 16))
DIRECT = 48
TURNS = (-1, 1)


def kernel(
    total,
    atoms_hbm, points_hbm, bead_hbm, count_hbm, type_hbm, ptype_hbm, targets_hbm,
    gram_out, rhs_out,
    atoms, points, units, kbuf, rbuf, sbuf, wbuf, acc, obuf, tbuf, relay,
    bead_in, count_in, type_in, ptype, targets_in, repeated, live,
    load_sem, k_send, k_recv, d_send, d_recv, s_send, s_recv, w_send, w_recv, o_send, o_recv, o_local, t_send, t_recv, y_send, y_recv, f_send, f_recv,
):
    width = points.shape[1]
    shard = points.shape[0]
    slots = BEADS * GROUP
    dp = lax.axis_index("dp")
    row = lax.axis_index("row")
    col = lax.axis_index("col")
    x, z = dp // SIDE, dp % SIDE
    h, core = row // 2, row % 2
    y = h * 2 + col
    at_strip = dp % 8
    owner = (dp // 8) == col

    def on_plane(step_x, step_z):
        return {"dp": ((x + step_x) % SIDE) * SIDE + (z + step_z) % SIDE, "row": row, "col": col}

    def on_x(step):
        return on_plane(step, 0)

    def on_z(step):
        return on_plane(0, step)

    def on_y(step, at_core):
        to = (y + step) % SIDE
        return {"dp": dp, "row": (to // 2) * 2 + at_core, "col": to % 2}

    sibling = on_y(0, 1 - core)
    up, down = on_y(1, core), on_y(-1, core)
    h_up, h_down = ((y + 1) % SIDE) // 2, ((y - 1) % SIDE) // 2
    offsets = [(i, j) for i in range(SIDE) for j in range(SIDE) if (i, j) != (0, 0)]

    loads = []
    compute_order = order = (0, 1, 2, 3)
    per_sub = SUB // GROUP
    small = []
    for i, (src, dst) in enumerate((
        (bead_hbm, bead_in), (count_hbm, count_in), (type_hbm, type_in), (ptype_hbm, ptype),
        (targets_hbm, targets_in),
    )):
        copy = pltpu.make_async_copy(src, dst, load_sem.at[5 + i])
        copy.start()
        small.append(copy)
    load_points = pltpu.make_async_copy(points_hbm, points, load_sem.at[4])
    load_points.start()
    for t in order:
        rows = pl.ds(t * per_sub, per_sub)
        copy = pltpu.make_async_copy(atoms_hbm.at[rows], atoms.at[rows], load_sem.at[t])
        if len(loads) < 1:
            copy.start()
        loads.append(copy)

    barrier = pltpu.get_barrier_semaphore()
    peers = [on_plane(*offset) for offset in offsets]
    peers += [sibling, up, down, on_y(2, core), on_y(2, 1 - core)]
    for peer in peers:
        pl.semaphore_signal(barrier, inc=1, device_id=peer, device_id_type=MESH)

    pending = []

    def remote(src, dst, send, recv, peer):
        return pltpu.make_async_remote_copy(
            src_ref=src, dst_ref=dst, send_sem=send, recv_sem=recv,
            device_id=peer, device_id_type=MESH,
        )

    def slot(route, outer, inner, sub):
        return kbuf.at[route, outer % SIDE, pl.ds((inner % SIDE) * HALF + sub * SUB, SUB), :]

    def recv_sem(route, outer, inner, sub):
        return k_recv.at[((route * SIDE + outer % SIDE) * SIDE + inner % SIDE) * 2 + sub]

    def along(route, phase, step):
        return on_x(step) if (route == 0) == (phase == 0) else on_z(step)

    def send(route, outer, inner, sub, phase, step):
        if phase == 0:
            to = (route, outer, inner - step, sub)
        else:
            to = (route, outer - step, inner, sub)
        copy = remote(
            slot(route, outer, inner, sub), slot(*to), k_send.at[len(pending)], recv_sem(*to),
            along(route, phase, step),
        )
        copy.start()
        pending.append(copy)

    def arrived(route, outer, inner, sub):
        here = slot(route, outer, inner, sub)
        remote(here, here, k_send.at[0], recv_sem(route, outer, inner, sub), sibling).wait_recv()

    def send_own(route, sub):
        for step in (1, -1):
            send(route, 0, 0, sub, 0, step)
        for step in (1, -1):
            send(route, 0, 0, sub, 1, step)

    def inner_step(route, inner, sub):
        arrived(route, 0, inner, sub)
        if inner == 3 and sub == 0:
            send(route, 0, inner, sub, 0, 1)
        if inner == 1 and sub == 1:
            send(route, 0, inner, sub, 0, -1)
        for step in (1, -1):
            send(route, 0, inner, sub, 1, step)

    def outer_step(route, inner, sub):
        if sub == 0:
            arrived(route, 3, inner, 0)
            send(route, 3, inner, 0, 1, 1)
        else:
            arrived(route, 1, inner, 1)
            send(route, 1, inner, 1, 1, -1)

    def near(route, sub):
        for inner in (3, 1) if sub == 0 else (1, 3):
            inner_step(route, inner, sub)
        outer_step(route, 0, sub)

    def middle(route, sub):
        inner_step(route, 2, sub)
        outer_step(route, 3, sub)
        outer_step(route, 1, sub)

    def far(route, sub):
        outer_step(route, 2, sub)

    def prepare():
        for copy in small:
            copy.wait()
        wbuf[0, 0] = jnp.zeros_like(wbuf[0, 0])
        wbuf[0, 0, 0:3, :] = jnp.concatenate([targets_in[:, 0], targets_in[:, 1]], axis=1)
        spread = lax.broadcasted_iota(jnp.int32, (ATOMS, 128), 1) % ATOMS
        spread = jnp.where(spread == lax.broadcasted_iota(jnp.int32, (ATOMS, 128), 0), 1.0, 0.0)
        for s in range(2):
            here = slice(s * HALF, (s + 1) * HALF)
            beads = bead_in[s].astype(jnp.float32).astype(jnp.bfloat16)
            repeated[here, :] = lax.dot_general(
                beads, spread.astype(jnp.bfloat16), (((0,), (0,)), ((), ())), preferred_element_type=jnp.float32
            )
            alive = lax.broadcasted_iota(jnp.int32, (BEADS, HALF), 0) < count_in[s:s + 1, :]
            kinds = jnp.where(alive, type_in[s], -1).astype(jnp.float32).astype(jnp.bfloat16)
            same = lax.broadcasted_iota(jnp.int32, (BEADS, BEADS), 0)
            same = same == lax.broadcasted_iota(jnp.int32, (BEADS, BEADS), 1)
            kinds = lax.dot_general(
                kinds, jnp.where(same, 1.0, 0.0).astype(jnp.bfloat16), (((0,), (0,)), ((), ())),
                preferred_element_type=jnp.float32,
            )
            for i in range(HALF // GROUP):
                rows = kinds[i * GROUP:(i + 1) * GROUP]
                for b in range(BEADS):
                    live[s * (HALF // GROUP) + i, b * GROUP:(b + 1) * GROUP, :] = jnp.broadcast_to(
                        rows[:, b:b + 1], (GROUP, 128)
                    )

    bead_id = (lax.broadcasted_iota(jnp.int32, (slots, GROUP * ATOMS), 0) // GROUP).astype(jnp.float32)
    member = lax.broadcasted_iota(jnp.int32, (GROUP, GROUP * ATOMS), 1) // ATOMS
    member = member == lax.broadcasted_iota(jnp.int32, (GROUP, GROUP * ATOMS), 0)

    def unit_points():
        def body(i, carry):
            rows = pl.ds(pl.multiple_of(i * 128, 128), 128)
            wide = points[rows, :].astype(jnp.float32)
            mean = jnp.sum(wide * wide, axis=1, keepdims=True) * (1.0 / width)
            points[rows, :] = (wide * lax.rsqrt(mean + EPSILON)).astype(jnp.bfloat16)
            return carry
        lax.fori_loop(0, shard // 128, body, 0)

    def unit_beads(t):
        for i in range(per_sub):
            j = t * per_sub + i
            near_atoms = repeated[j * GROUP:(j + 1) * GROUP, :]
            own = jnp.where(member, jnp.concatenate([near_atoms, near_atoms], axis=1), -1.0)
            onehot = jnp.where(jnp.concatenate([own] * BEADS, axis=0) == bead_id, 1.0, 0.0)
            size = jnp.maximum(jnp.sum(onehot, axis=1, keepdims=True), 1.0)
            summed = jnp.dot(onehot.astype(jnp.bfloat16), atoms[j], preferred_element_type=jnp.float32)
            inverse = 1.0 / size
            mean = jnp.sum(summed * summed, axis=1, keepdims=True) * (inverse * inverse * (1.0 / width))
            scale = inverse * lax.rsqrt(mean + EPSILON)
            units[compute_order.index(t) % 2, i * slots:(i + 1) * slots, :] = (summed * scale).astype(jnp.bfloat16)

    def kernel_rows(t):
        route, sub = t // 2, t % 2
        tile = 256
        for cols in (slice(i, i + tile) for i in range(0, shard, tile)):
            scores = lax.dot_general(
                units[compute_order.index(t) % 2], points[cols, :], (((1,), (1,)), ((), ())), preferred_element_type=jnp.float32,
            )
            kind = ptype[:, cols].astype(jnp.float32)
            parts = []
            for i in range(per_sub):
                j = t * per_sub + i
                part = jnp.exp2(scores[i * slots:(i + 1) * slots] * (LOG2E * width ** (-0.5)))
                alive = live[j]
                part = jnp.where(jnp.concatenate([alive] * (tile // 128), axis=1) == kind, part, 0.0)
                parts.append(jnp.sum(part.reshape(BEADS, GROUP, tile), axis=0))
            kbuf[route, 0, sub * SUB:(sub + 1) * SUB, cols] = jnp.concatenate(parts, axis=0).astype(jnp.bfloat16)

    groups = [(route, outer) for outer in (0, 3, 1, 2) for route in (0, 1)]
    index_of = {group: g for g, group in enumerate(groups)}

    def relative(route, step_x, step_z):
        return (step_z % SIDE, step_x % SIDE) if route == 0 else (step_x % SIDE, step_z % SIDE)

    def direct(route, n, to_x, to_z, s):
        outer, inner = relative(route, -to_x, -to_z)
        lanes = pl.ds(pl.multiple_of(s * STRIP, STRIP), STRIP)
        return remote(
            kbuf.at[route, 0, pl.ds(0, HALF), lanes],
            rbuf.at[route, outer, pl.ds(inner * HALF, HALF), :],
            d_send.at[route * 15 + n],
            d_recv.at[(route * SIDE + outer) * SIDE + inner],
            on_plane(to_x, to_z),
        )

    def direct_each(route, do):
        for n, (to_x, to_z) in enumerate(offsets):
            there_x, there_z = (x + to_x) % SIDE, (z + to_z) % SIDE

            @pl.when(there_x // 2 == col)
            def _():
                do(direct(route, n, to_x, to_z, (there_x % 2) * SIDE + there_z))

    def strip(g, r):
        return sbuf.at[g, pl.ds(pl.multiple_of(r * STRIP, STRIP), STRIP), :]

    def strip_copy(g, r, which, peer):
        here = strip(g, r)
        return remote(here, here, s_send.at[g * 4 + which], s_recv.at[g * 4 + r], peer)

    def strip_arrived(g, r):
        strip_copy(g, r, 0, sibling).wait_recv()

    def strip_send(group):
        g = index_of[group]
        route, outer = group

        @pl.when(owner)
        def _():
            for inner in range(SIDE):
                if (outer, inner) == (0, 0):
                    lanes = pl.ds(pl.multiple_of(at_strip * STRIP, STRIP), STRIP)
                    rbuf[route, 0, 0:HALF, :] = kbuf[route, 0, 0:HALF, lanes]
                else:
                    here = rbuf.at[route, outer, pl.ds(inner * HALF, HALF), :]
                    remote(
                        here, here, d_send.at[0], d_recv.at[(route * SIDE + outer) * SIDE + inner], sibling
                    ).wait_recv()
            sbuf[g, pl.ds(pl.multiple_of(row * STRIP, STRIP), STRIP), :] = rbuf[route, outer].T
            strip_copy(g, row, 0, up).start()
            strip_copy(g, row, 1, down).start()
            strip_copy(g, row, 2, sibling).start()

    def strip_relay(group):
        g = index_of[group]
        r_up, r_down = h_up * 2 + core, h_down * 2 + core

        @pl.when(jnp.logical_not(owner))
        def _():
            strip_arrived(g, r_down)
            strip_arrived(g, r_up)

            @pl.when(h == (g // 2) % 2)
            def _():
                strip_copy(g, r_down, 2, up).start()
                strip_copy(g, r_up, 3, down).start()
            strip_copy(g, r_down, 0, sibling).start()
            strip_copy(g, r_up, 1, sibling).start()

    def strip_last(group):
        g = index_of[group]
        other = (1 - h) * 2 + core

        @pl.when(owner)
        def _():
            strip_arrived(g, other)
            strip_copy(g, other, 3, sibling).start()

    def strip_drain(group):
        g = index_of[group]
        for which in range(2):
            strip_copy(g, row, which, sibling).wait_send()

        @pl.when(jnp.logical_or(owner, h == (g // 2) % 2))
        def _():
            for which in range(2, 4):
                strip_copy(g, row, which, sibling).wait_send()

    def strips_here(group):
        g = index_of[group]
        strip_arrived(g, 1 - core)
        strip_arrived(g, 2 + 1 - core)

    def gram(group, first=False):
        g = index_of[group]
        strips_here(group)
        route, outer = group
        tile = 256

        def body(ct, carry):
            cols = pl.ds(pl.multiple_of(ct * tile, tile), tile)
            part = jnp.dot(sbuf[g], kbuf[route, outer, :, cols], preferred_element_type=jnp.float32)
            if first:
                acc[:, cols] = part
            else:
                acc[:, cols] += part
            return carry
        lax.fori_loop(0, shard // tile, body, 0)

    def weight_copy(axis, step):
        if axis == 0:
            src, dst, peer = wbuf.at[0, 0], wbuf.at[0, (-step) % SIDE], on_x(step)
        else:
            src, dst, peer = wbuf.at[0], wbuf.at[(-step) % SIDE], on_z(step)
        i = axis * 3 + step - 1
        return remote(src, dst, w_send.at[i], w_recv.at[i], peer)

    def weight_rows():
        low = lax.broadcasted_iota(jnp.int32, (8, 128), 1) < HALF
        for (route, outer), g in index_of.items():
            if route == 0:
                parts = [wbuf[outer, i] for i in range(SIDE)]
                pairs = [jnp.where(low, parts[i], pltpu.roll(parts[i + 1], HALF, 1)) for i in (0, 2)]
            else:
                parts = [wbuf[i, outer] for i in range(SIDE)]
                pairs = [jnp.where(low, pltpu.roll(parts[i], HALF, 1), parts[i + 1]) for i in (0, 2)]
            wide = jnp.concatenate(pairs, axis=1)
            high = wide.astype(jnp.bfloat16).astype(jnp.float32)
            both = jnp.concatenate([high, wide - high], axis=0)
            sbuf[g, 4 * STRIP:, :] = both.astype(jnp.bfloat16)

    prepare()
    load_points.wait()
    for copy in loads[1:]:
        copy.start()
    unit_points()
    loads[0].wait()
    unit_beads(0)

    def compute(n):
        if n == 1:
            loads[1].wait()
            unit_beads(compute_order[1])
        if 0 < n < 3:
            loads[n + 1].wait()
            unit_beads(compute_order[n + 1])
        kernel_rows(compute_order[n])

    def gather_rest(route, outer):
        for inner in (0, 3, 1, 2):
            for sub in {0: (), 3: (1,), 1: (0,), 2: (0, 1)}[outer]:
                arrived(route, outer, inner, sub)

    compute(0)
    pl.semaphore_wait(barrier, len(peers))
    send_own(0, 0)
    compute(1)
    direct_each(0, lambda copy: copy.start())
    for step in (1, 2, 3):
        weight_copy(0, step).start()
    send_own(0, 1)
    compute(2)
    send_own(1, 0)
    compute(3)
    send_own(1, 1)
    direct_each(1, lambda copy: copy.start())
    strip_send((0, 1))
    strip_send((0, 2))
    strip_send((0, 0))
    strip_send((0, 3))
    near(1, 0)
    near(0, 0)
    strip_send((1, 0))
    strip_relay((0, 1))
    near(0, 1)
    strip_relay((0, 0))
    strip_relay((0, 2))
    near(1, 1)
    for step in (1, 2, 3):
        weight_copy(0, step).wait_recv()
    for step in (1, 2, 3):
        weight_copy(1, step).start()
    strip_relay((0, 3))
    strip_relay((1, 0))
    strip_send((1, 3))
    strip_send((1, 2))
    strip_send((1, 1))
    middle(1, 0)
    middle(0, 0)
    strip_relay((1, 3))
    strip_last((0, 0))
    middle(0, 1)
    strip_relay((1, 2))
    middle(1, 1)
    strip_relay((1, 1))
    strip_last((0, 1))
    strip_last((1, 0))
    for step in (1, 2, 3):
        weight_copy(1, step).wait_recv()
    weight_rows()
    gather_rest(0, 0)
    gram((0, 0), first=True)
    gather_rest(1, 0)
    gram((1, 0))
    far(1, 0)
    strip_last((0, 3))
    far(0, 1)
    strip_last((1, 3))
    strip_last((0, 2))
    far(0, 0)
    gather_rest(0, 1)
    gram((0, 1))
    far(1, 1)
    strip_last((1, 1))
    gather_rest(1, 3)
    gram((1, 3))
    strip_last((1, 2))
    gather_rest(0, 3)
    gram((0, 3))
    gather_rest(1, 1)
    gram((1, 1))
    for route in (0, 1):
        gather_rest(route, 2)
        strips_here((route, 2))

    def finish(rows, cols):
        value = acc[rows, cols]
        for route in (0, 1):
            g = index_of[(route, 2)]
            value += jnp.dot(sbuf[g, rows, :], kbuf[route, 2, :, cols], preferred_element_type=jnp.float32)
        return value * (1.0 / total)

    def block(r):
        rows = pl.ds(pl.multiple_of(r * STRIP, STRIP), STRIP)
        obuf[r] = finish(rows, pl.ds(0, shard)).astype(jnp.bfloat16)

    across = (1 - h) * 2

    def out_copy(r, which, peer):
        return remote(obuf.at[r], gram_out.at[row], o_send.at[which], o_recv.at[row], peer)

    def out_done(r, which):
        copy = remote(obuf.at[r], gram_out.at[r], o_send.at[which], o_recv.at[r], sibling)
        copy.wait_send()
        copy.wait_recv()

    def turned(s, k, do_remote, do_local):
        there = gram_out.at[across + k, :, pl.ds(pl.multiple_of(at_strip * STRIP, STRIP), STRIP)]

        @pl.when(dp != 8 * col + s)
        def _():
            peer = {"dp": 8 * col + s, "row": row, "col": col}
            do_remote(remote(tbuf.at[s, k], there, t_send.at[2 * s + k], t_recv.at[2 * at_strip + k], peer))

        @pl.when(dp == 8 * col + s)
        def _():
            do_local(pltpu.make_async_copy(tbuf.at[s, k], there, t_send.at[2 * s + k]))

    def turned_arrived(s, k):
        @pl.when(dp != 8 * col + s)
        def _():
            there = gram_out.at[across + k, :, pl.ds(s * STRIP, STRIP)]
            remote(tbuf.at[s, k], there, t_send.at[2 * s + k], t_recv.at[2 * s + k], sibling).wait_recv()

    def start(copy):
        copy.start()

    def turn(at_col):
        return TURNS[0] + (TURNS[1] - TURNS[0]) * at_col

    def straight(k):
        rows = pl.ds(DIRECT, STRIP - DIRECT)
        return remote(
            obuf.at[across + k, rows], gram_out.at[row, rows], o_send.at[k], o_recv.at[row], on_y(2, k)
        )

    def straight_done(k):
        rows = pl.ds(DIRECT, STRIP - DIRECT)
        copy = remote(
            obuf.at[across + k, rows], gram_out.at[across + k, rows], o_send.at[k], o_recv.at[across + k], sibling
        )
        copy.wait_send()
        copy.wait_recv()

    def first_leg(k, i):
        rows = pl.ds(*RELAYED[i])
        return remote(
            obuf.at[across + k, rows], relay.at[k, rows], y_send.at[2 * k + i], y_recv.at[2 * k + i],
            on_y(turn(col), core),
        )

    def second_leg(k, i):
        rows = pl.ds(*RELAYED[i])
        way = turn(1 - col)
        source = ((y - way + SIDE) % SIDE) // 2 * 2 + core
        return remote(
            relay.at[k, rows], gram_out.at[source, rows], f_send.at[2 * k + i], f_recv.at[2 * core + i],
            on_y(way, k),
        )

    def relayed_arrived(k, i):
        here = gram_out.at[across + k, pl.ds(*RELAYED[i])]
        remote(here, here, y_send.at[0], f_recv.at[2 * k + i], sibling).wait_recv()

    for k in range(2):
        block(across + k)

        @pl.when(jnp.logical_not(owner))
        def _():
            for i in range(2):
                first_leg(k, i).start()
            straight(k).start()

        @pl.when(owner)
        def _():
            for s in range(8):
                tbuf[s, k] = obuf[across + k, :, s * STRIP:(s + 1) * STRIP].T
                turned(s, k, start, start)
    block(h * 2 + 1 - core)
    out_copy(h * 2 + 1 - core, 2, sibling).start()

    @pl.when(owner)
    def _():
        for k in range(2):
            for i in range(2):
                first_leg(k, i).wait_recv()
                second_leg(k, i).start()
    block(row)
    keep = pltpu.make_async_copy(obuf.at[row], gram_out.at[row], o_local)
    keep.start()
    tail = finish(pl.ds(4 * STRIP, 16), pl.ds(0, shard))
    rhs_out[...] = tail[0:8] + tail[8:16]
    for copy in pending:
        copy.wait_send()
    for route in (0, 1):
        direct_each(route, lambda copy: copy.wait_send())
    for group in groups:
        strip_drain(group)
    for axis in (0, 1):
        for step in (1, 2, 3):
            weight_copy(axis, step).wait_send()
    keep.wait()
    out_done(h * 2 + 1 - core, 2)

    @pl.when(jnp.logical_not(owner))
    def _():
        for k in range(2):
            straight_done(k)
            for i in range(2):
                first_leg(k, i).wait_send()
                relayed_arrived(k, i)

    @pl.when(owner)
    def _():
        for k in range(2):
            for i in range(2):
                second_leg(k, i).wait_send()
        for s in range(8):
            for k in range(2):
                turned(s, k, lambda copy: copy.wait_send(), lambda copy: copy.wait())
                turned_arrived(s, k)


def widen(gram_in, rhs_in, gram_out, rhs_out):
    for q in range(4):
        gram_out[:, q, :] = gram_in[q].astype(jnp.float32)
    rhs_out[...] = rhs_in[0:3, :]


def shards(atom_feats, atom_bead, bead_count, bead_type, sparse_points, sparse_type, targets):
    slabs, local, atoms, width = atom_feats.shape
    config_rows = slabs * local
    shard = sparse_points.shape[0]
    total = config_rows * lax.axis_size("dp")
    blocks = config_rows // GROUP
    bf16, f32, i32 = jnp.bfloat16, jnp.float32, jnp.int32
    dma = pltpu.SemaphoreType.DMA
    vmem = pl.BlockSpec(memory_space=pltpu.VMEM)
    hbm = pl.BlockSpec(memory_space=pltpu.HBM)
    gram, rhs = pl.pallas_call(
        functools.partial(kernel, total),
        out_shape=(
            jax.ShapeDtypeStruct((4, STRIP, shard), bf16),
            jax.ShapeDtypeStruct((8, shard), f32),
        ),
        in_specs=[hbm] * 7,
        out_specs=(hbm, vmem),
        scratch_shapes=[
            pltpu.VMEM((blocks, GROUP * atoms, width), bf16),
            pltpu.VMEM((shard, width), bf16),
            pltpu.VMEM((2, SUB * BEADS, width), bf16),
            pltpu.VMEM((2, SIDE, SIDE * HALF, shard), bf16),
            pltpu.VMEM((2, SIDE, SIDE * HALF, STRIP), bf16),
            pltpu.VMEM((8, 4 * STRIP + 16, SIDE * HALF), bf16),
            pltpu.VMEM((SIDE, SIDE, 8, 128), f32),
            pltpu.VMEM((4 * STRIP + 16, shard), f32),
            pltpu.VMEM((4, STRIP, shard), bf16),
            pltpu.VMEM((8, 2, STRIP, STRIP), bf16),
            pltpu.VMEM((2, DIRECT, shard), bf16),
            pltpu.VMEM((slabs, atoms, local), i32),
            pltpu.VMEM(bead_count.shape, i32),
            pltpu.VMEM((slabs, BEADS, local), i32),
            pltpu.VMEM((1, shard), i32),
            pltpu.VMEM((3, slabs, local), f32),
            pltpu.VMEM((config_rows, 128), f32),
            pltpu.VMEM((blocks, BEADS * GROUP, 128), f32),
            dma((10,)),
            dma((60,)),
            dma((64,)),
            dma((30,)),
            dma((32,)),
            dma((32,)),
            dma((32,)),
            dma((6,)),
            dma((6,)),
            dma((3,)),
            dma((4,)),
            dma,
            dma((16,)),
            dma((16,)),
            dma((4,)),
            dma((4,)),
            dma((4,)),
            dma((4,)),
        ],
        compiler_params=pltpu.CompilerParams(
            collective_id=0, has_side_effects=True, vmem_limit_bytes=60 * 1024 * 1024
        ),
    )(
        atom_feats.reshape(blocks, GROUP * atoms, width), sparse_points, jnp.swapaxes(atom_bead, 1, 2),
        bead_count, jnp.swapaxes(bead_type, 1, 2), sparse_type.reshape(1, shard), jnp.swapaxes(targets, 0, 1),
    )
    steps = 2
    return pl.pallas_call(
        widen,
        grid=(steps,),
        out_shape=(
            jax.ShapeDtypeStruct((STRIP, 4, shard), f32),
            jax.ShapeDtypeStruct((3, shard), f32),
        ),
        in_specs=[
            pl.BlockSpec((4, STRIP // steps, shard), lambda i: (0, i, 0)),
            pl.BlockSpec((8, shard), lambda i: (0, 0)),
        ],
        out_specs=(
            pl.BlockSpec((STRIP // steps, 4, shard), lambda i: (i, 0, 0)),
            pl.BlockSpec((3, shard), lambda i: (0, 0)),
        ),
        compiler_params=pltpu.CompilerParams(vmem_limit_bytes=60 * 1024 * 1024),
    )(gram, rhs)


def solution(mesh):
    return jax.shard_map(
        shards,
        mesh=mesh,
        in_specs=(
            P(None, "dp", None, None),
            P(None, "dp", None),
            P(None, "dp"),
            P(None, "dp", None),
            P(("row", "col"), None),
            P(("row", "col")),
            P(None, None, "dp"),
        ),
        out_specs=(P(("row", "dp"), None, "col"), P(None, ("row", "col"))),
        check_vma=False,
    )
```
